512 devices in a mesh: rep: 8 (over x, y_lo), exp: 64 (over z, y_hi, core).
Axes of the slice: x: 4, y: 4 (y_hi: 2, y_lo: 2; y = y_hi * 2 + y_lo), z: 16, core: 2. Of those that a mesh axis runs over, the one named last changes fastest.
Arguments:
- hidden_in: bfloat16 [8192, 2048], P('exp', 'rep'), may hold values from -36 to 36
- norm_gain: float32 [2048], replicated, may hold values from 0.25 to 1.75
- route_ids: int32 [8192, 2], P('exp'), may hold values from 0 to 63, all different within a row; in each aligned block of 128 rows (0 to 127, 128 to 255, ...) at most 5 rows name the same one
- route_weights: float32 [8192, 2], P('exp'), may hold values from 0.05 to 0.6
- w_gate: bfloat16 [64, 1536, 2048], P('exp', 'rep'), may hold values from -0.125 to 0.125
- w_up: bfloat16 [64, 1536, 2048], P('exp', 'rep'), may hold values from -0.125 to 0.125
- w_down: bfloat16 [64, 1536, 2048], P('exp', 'rep'), may hold values from -0.15625 to 0.15625
- out_grad: bfloat16 [8192, 2048], P('exp', 'rep'), may hold values from -6 to 6
Outputs:
- layer_out: bfloat16 [8192, 2048], P(('exp', 'rep'))
- input_grad: bfloat16 [8192, 2048], P(('exp', 'rep'))
- route_grad: float32 [8192, 2], P(('exp', 'rep'))
- gate_update: bfloat16 [64, 1536, 2048], P('exp', 'rep')
- up_update: bfloat16 [64, 1536, 2048], P('exp', 'rep')
- down_update: bfloat16 [64, 1536, 2048], P('exp', 'rep')
The draws below stay inside these ranges and needn't reach their ends.
Inputs may be any that keep to these rules, and one draw needn't show every extreme that they name: `route_ids`: each row names 2 different experts. Within each aligned block of 128 rows (the tokens of one index of exp) no expert is named by more than 5 rows, and in every draw some expert is named by exactly 5 rows of some block.
All inputs are finite; a program needn't handle non-finite values.
Results may differ from the reference program's by a relative error of at most 0.02.
Values may be sent and summed in bfloat16 or wider, within the bound.
A program may use at most 64 MiB of HBM per device.

```python
import math
import jax
import jax.numpy as jnp
import numpy as np
from jax import lax

D = 2048
FF = 1536
TOPK = 2
TOK_DEV = 128
EXPERTS = 64
TOKENS = 8192
CAP = 5
N_REP = 8


def draw_hidden_in(key, part):
    key = jax.random.fold_in(key, 11)
    first, second, third = jax.random.split(key, 3)
    base = jnp.clip(jax.random.normal(first, (TOKENS, D), jnp.float32), -4.0, 4.0)
    row_scale = jnp.exp(jax.random.uniform(second, (TOKENS, 1), jnp.float32, math.log(0.3), math.log(3.0)))
    column_scale = jnp.exp(jax.random.uniform(third, (1, D), jnp.float32, math.log(0.3), math.log(3.0)))
    return (base * row_scale * column_scale).astype(jnp.bfloat16)


def shard_levels(own_key, extent, shards, smallest, largest):
    def one(dim, parts):
        heights = jax.random.uniform(jax.random.fold_in(jax.random.fold_in(own_key, 6), dim), (parts,), jnp.float32, smallest / len(shards), largest / len(shards))
        return jnp.repeat(jnp.exp(heights), extent[dim] // parts).reshape((-1,) + (1,) * (len(extent) - dim - 1))

    loudness = one(*shards[0])
    for cut in shards[1:]:
        loudness = loudness * one(*cut)
    return loudness


def shared_out(key, own, number, rows, count, top, limit, lean):
    ranking = jax.random.permutation(key, count)
    heavy_load, ordinary = load_shares(count, rows * top, limit, lean, True), load_shares(count, rows * top, limit, lean, False)
    places = jnp.arange(count)

    def named(sizes, rotation):
        used = int((sizes > 0).sum())
        fixed = max(1, used // 4)
        shifted = fixed + (places - fixed + rotation * (used - fixed)) % max(1, count - fixed)
        return jnp.zeros((count,), jnp.int32).at[ranking[jnp.where(places < fixed, places, shifted)]].set(jnp.asarray(sizes, jnp.int32))

    sizes = jnp.where(number % 4 == 0, named(heavy_load, number // 4), named(ordinary, number - number // 4 - 1))
    mixed = jax.random.permutation(jax.random.fold_in(own, 3), count)
    source_of, receiver = mixed[0:count // 2 * 2:2], mixed[1:count // 2 * 2:2]
    room = jnp.minimum(sizes[source_of] - 1, limit - sizes[receiver]) // 2
    room = jnp.where((source_of == ranking[0]) | (receiver == ranking[0]) | (sizes[receiver] == 0), 0, jnp.maximum(room, 0))
    shifted = jax.random.randint(jax.random.fold_in(own, 4), (count // 2,), 0, 1 << 20) % (room + 1)
    sizes = sizes.at[source_of].add(-shifted).at[receiver].add(shifted)
    items = jnp.searchsorted(jnp.cumsum(sizes), jnp.arange(rows * top), side="right").astype(jnp.int32)
    grid = items.reshape(top, rows).T
    grid = grid[jax.random.permutation(jax.random.fold_in(own, 1), rows)]
    rotation = jax.random.randint(jax.random.fold_in(own, 2), (rows, 1), 0, top)
    return jnp.take_along_axis(grid, (jnp.arange(top)[None, :] + rotation) % top, axis=1)


def load_shares(amount, total, bound, lean, full):
    portions = [(1 << 20) // math.isqrt(rank ** lean) + 1 for rank in range(1, amount + 1)]
    largest = bound if full else min(bound, max(-(-total // amount), total * portions[0] // sum(portions)))
    least = 1 if total - largest >= amount - 1 else 0
    counts, spare = [largest] + [least] * (amount - 1), total - largest - least * (amount - 1)
    while spare > 0:
        candidates = [i for i in range(1, amount) if counts[i] < largest] or [i for i in range(1, amount) if counts[i] < bound]
        pool, budget = sum([portions[i] for i in candidates]), spare
        for i in candidates:
            more = min(bound - counts[i], max(1, budget * portions[i] // pool), spare)
            counts[i] = counts[i] + more
            spare = spare - more
    return np.array(counts)


def bell_draw(stream_key, dims, scale, limit, cuts=(), held_as=jnp.bfloat16):
    array = scale * jax.random.normal(stream_key, dims, jnp.float32)
    if cuts:
        array = array * shard_levels(stream_key, dims, cuts, -0.22, 0.18)
    return jnp.clip(array, -limit, limit).astype(held_as)


def setup_inputs(seed: int = 0) -> dict:
    seeds = jax.random.split(jax.random.key(seed), 9)
    hidden_in = draw_hidden_in(jax.random.fold_in(seeds[8], 71), 0)
    norm_gain = jnp.clip(1.0 + 0.15 * jax.random.normal(seeds[1], (D,), jnp.float32), 0.25, 1.75)
    route_ids_keys = jax.random.split(jax.random.fold_in(seeds[2], 1), TOKENS // TOK_DEV)
    route_ids_turns = jax.random.permutation(jax.random.fold_in(seeds[2], 3), TOKENS // TOK_DEV)
    route_ids = jax.vmap(lambda own, number: shared_out(jax.random.fold_in(seeds[2], 2), own, number, TOK_DEV, EXPERTS, TOPK, CAP, 2))(route_ids_keys, route_ids_turns).reshape((TOKENS, TOPK))
    route_weights = jnp.clip(jnp.exp(math.log(0.6) - 2.4849067 * jax.random.uniform(seeds[3], (TOKENS, TOPK), jnp.float32) ** shard_levels(seeds[3], (TOKENS, TOPK), ((0, 64),), -0.2, 0.2)), 0.05, 0.6)
    w_gate = bell_draw(seeds[4], (EXPERTS, FF, D), D ** -0.5, 0.125, ((0, 64), (1, 8)))
    w_up = bell_draw(seeds[5], (EXPERTS, FF, D), D ** -0.5, 0.125, ((0, 64), (1, 8)))
    w_down = bell_draw(seeds[6], (EXPERTS, FF, D), FF ** -0.5, 0.15625, ((0, 64), (1, 8)))
    out_grad = bell_draw(seeds[7], (TOKENS, D), 1.0, 6.0, ((0, 64), (1, 8)))
    return {"hidden_in": hidden_in, "norm_gain": norm_gain, "route_ids": route_ids, "route_weights": route_weights, "w_gate": w_gate, "w_up": w_up, "w_down": w_down, "out_grad": out_grad}


epsilon = 1e-06

def expert_pass(operands):
    rows_normed, rows_grad, gate_matrix, up_matrix, down_matrix = operands
    row_total = rows_normed.shape[0]
    hidden_count, feature_count = gate_matrix.shape
    block_width = hidden_count // N_REP
    contract_last = (((1,), (1,)), ((), ()))
    gate_pre = lax.dot_general(rows_normed, gate_matrix, contract_last, preferred_element_type=jnp.float32)
    up_pre = lax.dot_general(rows_normed, up_matrix, contract_last, preferred_element_type=jnp.float32)
    sigmoid_gate = jax.nn.sigmoid(gate_pre)
    activated = gate_pre * sigmoid_gate
    hidden = (activated * up_pre).astype(jnp.bfloat16)
    hidden_blocks = hidden.astype(jnp.float32).reshape(row_total, N_REP, block_width)
    down_blocks = down_matrix.astype(jnp.float32).reshape(N_REP, block_width, feature_count)
    out_parts = jnp.einsum('rnh,nhd->rnd', hidden_blocks, down_blocks, precision=lax.Precision.HIGHEST)
    out_parts = lax.optimization_barrier(out_parts.astype(jnp.bfloat16)).astype(jnp.float32)
    expert_out = lax.optimization_barrier(jnp.sum(out_parts, axis=1))
    hidden_grad = lax.dot_general(rows_grad, down_matrix, contract_last, preferred_element_type=jnp.float32)
    gate_grad = (hidden_grad * up_pre * sigmoid_gate * (1.0 + gate_pre * (1.0 - sigmoid_gate))).astype(jnp.bfloat16)
    up_grad = (hidden_grad * activated).astype(jnp.bfloat16)
    gate_blocks = gate_matrix.astype(jnp.float32).reshape(N_REP, block_width, feature_count)
    up_blocks = up_matrix.astype(jnp.float32).reshape(N_REP, block_width, feature_count)
    input_parts = jnp.einsum('rnh,nhd->rnd', gate_grad.astype(jnp.float32).reshape(row_total, N_REP, block_width), gate_blocks, precision=lax.Precision.HIGHEST)
    input_parts = input_parts + jnp.einsum('rnh,nhd->rnd', up_grad.astype(jnp.float32).reshape(row_total, N_REP, block_width), up_blocks, precision=lax.Precision.HIGHEST)
    input_parts = lax.optimization_barrier(input_parts.astype(jnp.bfloat16)).astype(jnp.float32)
    input_rows = lax.optimization_barrier(jnp.sum(input_parts, axis=1))
    contract_rows = (((0,), (0,)), ((), ()))
    down_update = lax.dot_general(hidden, rows_grad, contract_rows, preferred_element_type=jnp.float32).astype(jnp.bfloat16)
    gate_update = lax.dot_general(gate_grad, rows_normed, contract_rows, preferred_element_type=jnp.float32).astype(jnp.bfloat16)
    up_update = lax.dot_general(up_grad, rows_normed, contract_rows, preferred_element_type=jnp.float32).astype(jnp.bfloat16)
    return (expert_out, input_rows, gate_update, up_update, down_update)

def reference(hidden_in, norm_gain, route_ids, route_weights, w_gate, w_up, w_down, out_grad):
    token_total, feature_count = hidden_in.shape
    fanout = route_ids.shape[1]
    expert_count = w_gate.shape[0]
    block_count = token_total // TOK_DEV
    inputs_f32 = hidden_in.astype(jnp.float32)
    root_mean = jnp.sqrt(lax.optimization_barrier(jnp.mean(inputs_f32 * inputs_f32, axis=1, keepdims=True)) + epsilon)
    normed = (inputs_f32 * norm_gain[None, :] / root_mean).astype(jnp.bfloat16)
    expert_range = jnp.arange(expert_count, dtype=jnp.int32)
    per_expert = lax.optimization_barrier(jnp.sum((route_ids[:, :, None] == expert_range[None, None, :]).astype(jnp.int32), axis=1))
    blocked = per_expert.reshape(block_count, TOK_DEV, expert_count)
    earlier = (jnp.cumsum(blocked, axis=1) - blocked).reshape(token_total, expert_count)
    slot_index = jnp.take_along_axis(earlier, route_ids, axis=1)
    block_of = (jnp.arange(token_total, dtype=jnp.int32) // TOK_DEV).astype(jnp.int32)
    position = ((route_ids * block_count + block_of[:, None]) * CAP + slot_index).astype(jnp.int32)
    slot_total = expert_count * block_count * CAP
    source_route = jnp.full((slot_total,), -1, jnp.int32).at[position.reshape(-1)].set(jnp.arange(token_total * fanout, dtype=jnp.int32))
    filled = source_route >= 0
    route_safe = jnp.maximum(source_route, 0)
    token_safe = route_safe // fanout
    weight_rows = jnp.where(filled, route_weights.reshape(-1)[route_safe], jnp.zeros((), jnp.float32))
    rows_normed = jnp.where(filled[:, None], normed[token_safe], jnp.zeros((), jnp.bfloat16))
    rows_grad = (weight_rows[:, None] * out_grad[token_safe].astype(jnp.float32)).astype(jnp.bfloat16)
    row_shape = (expert_count, block_count * CAP, feature_count)
    expert_out, input_rows, gate_update, up_update, down_update = lax.map(expert_pass, (rows_normed.reshape(row_shape), rows_grad.reshape(row_shape), w_gate, w_up, w_down))
    picked_out = expert_out.reshape(slot_total, feature_count)[position]
    picked_input = input_rows.reshape(slot_total, feature_count)[position]
    layer_out = (inputs_f32 + lax.optimization_barrier(jnp.sum(route_weights[:, :, None] * picked_out, axis=1))).astype(jnp.bfloat16)
    route_grad = lax.optimization_barrier(jnp.sum(picked_out * out_grad.astype(jnp.float32)[:, None, :], axis=2))
    normed_grad = lax.optimization_barrier(jnp.sum(picked_input, axis=1))
    scaled = norm_gain[None, :] * normed_grad
    inner = lax.optimization_barrier(jnp.sum(scaled * inputs_f32, axis=1, keepdims=True))
    input_grad = (scaled / root_mean - inputs_f32 * inner / (feature_count * root_mean ** 3)).astype(jnp.bfloat16)
    return (layer_out, input_grad, route_grad, gate_update, up_update, down_update)
```

```python
import functools

import jax
import jax.numpy as jnp
from jax import lax
from jax.experimental import pallas as pl
from jax.experimental.pallas import tpu as pltpu
from jax.sharding import PartitionSpec as P

MESH = pl.DeviceIdType.MESH
EPSILON = 1e-06
NZ = 16
NJ = 4
WIDTH = 256
CHUNKS = 5
ROWS = 64
F32 = jnp.float32
BF16 = jnp.bfloat16


def z_offset(c, m):
    if m == 0:
        return c + 1
    if m == 1:
        return 15 - c
    if m == 2:
        return 8 - c
    return jnp.where(c == 0, 0, 8 + c)


def offset_rows(place):
    c, m = place >> 2, place & 3
    far = jnp.where(c == 0, 0, 8 + c)
    return jnp.where(m == 0, c + 1, jnp.where(m == 1, 15 - c, jnp.where(m == 2, 8 - c, far)))


def iota(shape, dim):
    return lax.broadcasted_iota(jnp.int32, shape, dim)


def dot(a, b, dims):
    return lax.dot_general(a, b, ((dims[:1], dims[1:]), ((), ())), preferred_element_type=F32)


def kernel(
    h_ref, g_ref, ids_ref, wrow_ref, wcol_ref, gain_ref, wg_hbm, wu_hbm, wd_hbm,
    lo_ref, ig_ref, rg_ref, gu_hbm, uu_hbm, du_hbm,
    wg, wu, wd, gu, uu, du,
    tokh, tokg, meta, hx, zmain, zleft, leftin, gat, nrm, par, got, fmain, fleft,
    fmain_in, fleft_in, loc, loc_in, fin, fin_in, hid, ggr, ugr, ht, ggt, ugt,
    w_sem, o_sem, tok_send, tok_recv, hx_send, hx_recv, zm_send, zm_recv, zl_send, zl_recv,
    c_send, c_recv, e_send, e_recv, fm_send, fm_recv, fl_send, fl_recv, l_send, l_recv, y_send, y_recv,
):
    reps = lax.axis_size("rep")
    features = reps * WIDTH
    share = h_ref.shape[0] // reps
    rep = lax.axis_index("rep")
    exp = lax.axis_index("exp")
    z, j = exp // NJ, exp % NJ

    def at_z(off):
        return {"exp": lax.rem(z + off, NZ) * NJ + j}

    def at_j(d):
        return {"exp": z * NJ + lax.rem(j + d, NJ)}

    def at_j_back(d):
        return {"exp": z * NJ + lax.rem(j + NJ - d, NJ)}

    def at_rep(ro):
        return {"rep": lax.rem(rep + ro, reps)}

    def send(src, dst, ssem, rsem, device):
        pltpu.make_async_remote_copy(
            src_ref=src, dst_ref=dst, send_sem=ssem, recv_sem=rsem, device_id=device, device_id_type=MESH
        ).start()

    def wait(ref, sem):
        pltpu.make_async_copy(ref, ref, sem).wait()

    weights = [
        pltpu.make_async_copy(wg_hbm, wg, w_sem.at[0]),
        pltpu.make_async_copy(wu_hbm, wu, w_sem.at[1]),
        pltpu.make_async_copy(wd_hbm, wd, w_sem.at[2]),
    ]
    for copy in weights:
        copy.start()

    barrier = pltpu.get_barrier_semaphore()

    def greet(off, carry):
        pl.semaphore_signal(barrier, inc=1, device_id=at_z(off), device_id_type=MESH)
        return carry

    lax.fori_loop(1, NZ, greet, 0)
    for d in range(1, NJ):
        pl.semaphore_signal(barrier, inc=1, device_id=at_j(d), device_id_type=MESH)
    for ro in range(1, reps):
        pl.semaphore_signal(barrier, inc=1, device_id=at_rep(ro), device_id_type=MESH)

    ids = ids_ref[...]
    expert_rows = iota((NZ * NJ, 128), 0)
    hits = [(expert_rows == ids[k : k + 1, :]).astype(F32) for k in range(2)]
    before = (iota((128, 128), 0) < iota((128, 128), 1)).astype(F32).astype(BF16)
    earlier = dot((hits[0] + hits[1]).astype(BF16), before, (1, 0))
    for k in range(2):
        number = jnp.sum(hits[k] * earlier, axis=0, keepdims=True)
        meta[0, k : k + 1, :] = ids[k : k + 1, :].astype(F32) * 8.0 + number
    meta[0, 2:4, :] = wrow_ref[...]

    pl.semaphore_wait(barrier, NZ - 1 + NJ - 1 + reps - 1)

    for d in range(1, NJ):
        send(meta.at[0], meta.at[d], tok_send.at[0], tok_recv.at[0, d], at_j(d))
        send(h_ref, tokh.at[d], tok_send.at[1], tok_recv.at[1, d], at_j(d))
        send(g_ref, tokg.at[d], tok_send.at[2], tok_recv.at[2, d], at_j(d))
    own_rows = pl.ds(pl.multiple_of(rep * share, 16), share)
    for ro in range(1, reps):
        to = pl.multiple_of(lax.rem(rep + ro, reps) * share, 16)
        send(h_ref.at[pl.ds(to, share), :], hx.at[rep], hx_send, hx_recv, at_rep(ro))
    hx[rep] = h_ref[own_rows, :]
    tokh[0] = h_ref[...]
    tokg[0] = g_ref[...]
    for d in range(1, NJ):
        wait(meta.at[d], tok_recv.at[0, d])
        wait(tokh.at[d], tok_recv.at[1, d])
        wait(tokg.at[d], tok_recv.at[2, d])

    def pick(code, block):
        rows_h = rows_g = weight = None
        for d in range(NJ):
            mine = jnp.where(block == d, code, -1.0)
            one = [mine == meta[d, k : k + 1, :] for k in range(2)]
            both = (one[0] | one[1]).astype(F32).astype(BF16)
            w = jnp.sum(
                jnp.where(one[0], meta[d, 2:3, :], 0.0) + jnp.where(one[1], meta[d, 3:4, :], 0.0), axis=1, keepdims=True
            )
            h, g = dot(both, tokh[d], (1, 0)), dot(both, tokg[d], (1, 0))
            rows_h = h if d == 0 else rows_h + h
            rows_g = g if d == 0 else rows_g + g
            weight = w if d == 0 else weight + w
        return rows_h.astype(BF16), (weight * rows_g).astype(BF16)

    def code_of(place, number):
        plane = (z + offset_rows(place)) & (NZ - 1)
        return ((plane * NJ + j) * 8 + number).astype(F32)

    for c in range(4):
        r = iota((ROWS, 1), 0)
        rows_h, rows_g = pick(code_of(4 * c + (r >> 4), r & 3), (r >> 2) & 3)
        zmain[c * ROWS : (c + 1) * ROWS, 0:WIDTH] = rows_h
        zmain[c * ROWS : (c + 1) * ROWS, WIDTH : 2 * WIDTH] = rows_g
        for m in range(4):
            if c == 0 and m == 3:
                gat[0, rep, 48:64, :] = zmain[48:64, :]
                continue
            off = z_offset(c, m) if m < 3 else 8 + c
            send(
                zmain.at[c * ROWS + 16 * m : c * ROWS + 16 * m + 16, :],
                gat.at[c, rep, 16 * m : 16 * m + 16, :],
                zm_send, zm_recv.at[c], at_z(off),
            )

    def spread(part, to_blocks):
        r, t = iota((ROWS, 4 * ROWS), 0), iota((ROWS, 4 * ROWS), 1)
        place, block = (r & 15, r >> 4) if to_blocks else (r >> 2, r & 3)
        return (t == 16 * place + 4 * part + block).astype(F32).astype(BF16)

    def to_tiles(rows):
        tiles = None
        for part in range(4):
            one = dot(spread(part, False), rows[:, 128 * part : 128 * part + 128], (0, 0))
            tiles = one if part == 0 else tiles + one
        return tiles.astype(BF16)

    r = iota((ROWS, 1), 0)
    rows_h, rows_g = pick(code_of(r >> 2, 4), r & 3)
    zleft[...] = to_tiles(jnp.concatenate([rows_h, rows_g], axis=1))
    leftin[48:64, :] = zleft[48:64, :]

    def send_left(src, dst, ssem, rsem, sign):
        for c in range(4):
            for m in range(4):
                if c == 0 and m == 3:
                    continue
                off = z_offset(c, m) if m < 3 else 8 + c
                at = slice(16 * (4 * c + m), 16 * (4 * c + m) + 16)
                send(src.at[at, :], dst.at[at, :], ssem, rsem, at_z(off if sign > 0 else NZ - off))

    send_left(zleft, leftin, zl_send, zl_recv, 1)

    def gather(c):
        for ro in range(1, reps):
            send(gat.at[c, rep], gat.at[c, rep], c_send.at[c], c_recv.at[c], at_rep(ro))

    def arrive(c):
        here = 48 if isinstance(c, int) and c == 0 else ROWS
        wait(gat.at[c, rep, 0:here, :], zm_recv.at[c])
        gather(c)

    def arrive_left():
        wait(leftin.at[0:240], zl_recv)
        for part in range(4):
            gat[4, rep, :, 128 * part : 128 * part + 128] = dot(spread(part, False), leftin[...], (1, 0)).astype(BF16)
        gather(4)

    def compute(c):
        wait(gat.at[c, pl.ds(0, reps - 1)], c_recv.at[c])
        squares = None
        for s in range(reps):
            x = gat[c, s, :, 0:WIDTH].astype(F32)
            part = jnp.sum(x * x, axis=1, keepdims=True)
            squares = part if s == 0 else squares + part
        scale = 1.0 / jnp.sqrt(squares / features + EPSILON)
        hidden_grad = None
        for s in range(reps):
            cols = slice(WIDTH * s, WIDTH * s + WIDTH)
            x = gat[c, s, :, 0:WIDTH].astype(F32)
            nrm[c, :, cols] = (x * gain_ref[:, cols] * scale).astype(BF16)
            part = dot(gat[c, s, :, WIDTH : 2 * WIDTH], wd[:, cols], (1, 1))
            hidden_grad = part if s == 0 else hidden_grad + part
        gate_pre = dot(nrm[c], wg[...], (1, 1))
        up_pre = dot(nrm[c], wu[...], (1, 1))
        sig = jax.nn.sigmoid(gate_pre)
        activated = gate_pre * sig
        hidden = (activated * up_pre).astype(BF16)
        gate_grad = (hidden_grad * up_pre * sig * (1.0 + gate_pre * (1.0 - sig))).astype(BF16)
        up_grad = (hidden_grad * activated).astype(BF16)
        hid[c], ggr[c], ugr[c] = hidden, gate_grad, up_grad
        for s in range(reps):
            cols = slice(WIDTH * s, WIDTH * s + WIDTH)
            par[c, s, :, 0:WIDTH] = dot(hidden, wd[:, cols], (1, 0)).astype(BF16)
            par[c, s, :, WIDTH : 2 * WIDTH] = (
                dot(gate_grad, wg[:, cols], (1, 0)) + dot(up_grad, wu[:, cols], (1, 0))
            ).astype(BF16)
        for ro in range(1, reps):
            send(par.at[c, lax.rem(rep + ro, reps)], got.at[c, rep], e_send.at[c], e_recv.at[c], at_rep(ro))
        got[c, rep] = par[c, rep]

    def reduced(c):
        wait(got.at[c, pl.ds(0, reps - 1)], e_recv.at[c])
        total = got[c, 0].astype(F32)
        for s in range(1, reps):
            total = total + got[c, s].astype(F32)
        return total.astype(BF16)

    def back(c):
        start = pl.multiple_of(c * ROWS, ROWS)
        fmain[pl.ds(start, ROWS), :] = reduced(c)
        for m in range(4):
            at = pl.ds(pl.multiple_of(start + 16 * m, 16), 16)

            def far(at=at, m=m):
                off = z_offset(c, m) if m < 3 else 8 + c
                send(fmain.at[at, :], fmain_in.at[at, :], fm_send, fm_recv, at_z(NZ - off))

            if m < 3:
                far()
            else:
                pl.when(c > 0)(far)

    for copy in weights:
        copy.wait()
    arrive(0)
    arrive(1)

    def tick(t, carry):
        compute(t)

        @pl.when(t < 2)
        def _():
            arrive(t + 2)

        @pl.when(t == 2)
        def _():
            arrive_left()

        @pl.when(t > 0)
        def _():
            back(t - 1)

        return carry

    lax.fori_loop(0, CHUNKS, tick, 0)

    def turned(ref):
        return jnp.transpose(ref[...].reshape(CHUNKS * ROWS, ref.shape[2]).astype(F32)).astype(BF16)

    ht[...], ggt[...], ugt[...] = turned(hid), turned(ggr), turned(ugr)
    for s in range(reps):
        cols = slice(WIDTH * s, WIDTH * s + WIDTH)
        rows_n = nrm[:, :, cols].reshape(CHUNKS * ROWS, WIDTH)
        rows_g = gat[:, s, :, WIDTH : 2 * WIDTH].reshape(CHUNKS * ROWS, WIDTH)
        gu[:, cols] = dot(ggt[...], rows_n, (1, 0)).astype(BF16)
        uu[:, cols] = dot(ugt[...], rows_n, (1, 0)).astype(BF16)
        du[:, cols] = dot(ht[...], rows_g, (1, 0)).astype(BF16)
    updates = [
        pltpu.make_async_copy(gu, gu_hbm, o_sem.at[0]),
        pltpu.make_async_copy(uu, uu_hbm, o_sem.at[1]),
        pltpu.make_async_copy(du, du_hbm, o_sem.at[2]),
    ]
    for copy in updates:
        copy.start()

    fleft[...] = to_tiles(reduced(4))
    fleft_in[48:64, :] = fleft[48:64, :]
    send_left(fleft, fleft_in, fl_send, fl_recv, -1)

    fmain_in[48:64, :] = fmain[48:64, :]
    wait(fmain_in.at[0:240, :], fm_recv)
    r, t = iota((4 * ROWS, 4 * ROWS), 0), iota((4 * ROWS, 4 * ROWS), 1)
    regroup = (t == 16 * ((r >> 2) & 15) + 4 * (r >> 6) + (r & 3)).astype(F32).astype(BF16)
    main = dot(regroup, fmain_in[...], (1, 0)).astype(BF16)
    loc_in[0, 0:64, :] = main[0:64, :]
    for d in range(1, NJ):
        loc[d, 0:64, :] = main[64 * d : 64 * d + 64, :]
        send(loc.at[d, 0:64, :], loc_in.at[d, 0:64, :], l_send.at[0], l_recv.at[0, d], at_j_back(d))
    wait(fleft_in.at[0:240, :], fl_recv)
    for part in range(4):
        cols = slice(128 * part, 128 * part + 128)
        fifth = dot(spread(part, True), fleft_in[...], (1, 0)).astype(BF16)
        loc_in[0, 64:80, cols] = fifth[0:16, :]
        for d in range(1, NJ):
            loc[d, 64:80, cols] = fifth[16 * d : 16 * d + 16, :]
    for d in range(1, NJ):
        send(loc.at[d, 64:80, :], loc_in.at[d, 64:80, :], l_send.at[1], l_recv.at[1, d], at_j_back(d))

    r = iota((80, 1), 0)
    place = jnp.where(r < 64, r >> 2, r - 64)
    number = jnp.where(r < 64, r & 3, 4)
    plane = (z + offset_rows(place)) & (NZ - 1)
    for d in range(1, NJ):
        wait(loc_in.at[d, 0:64, :], l_recv.at[0, d])
        wait(loc_in.at[d, 64:80, :], l_recv.at[1, d])
    picked = [None, None]
    for d in range(NJ):
        code = ((plane * NJ + ((j + d) & (NJ - 1))) * 8 + number).astype(F32)
        for k in range(2):
            one = (code == meta[0, k : k + 1, :]).astype(F32).astype(BF16)
            part = dot(one, loc_in[d], (0, 0))
            picked[k] = part if d == 0 else picked[k] + part
    grad = g_ref[...].astype(F32)
    out_rows = [p[:, 0:WIDTH] for p in picked]
    share_out = (wcol_ref[:, 0:1] * out_rows[0] + wcol_ref[:, 1:2] * out_rows[1]).astype(BF16)
    share_in = (picked[0][:, WIDTH:] + picked[1][:, WIDTH:]).astype(BF16)
    dots = [jnp.sum(p * grad, axis=1, keepdims=True) for p in out_rows]
    high = [d.astype(BF16).astype(F32) for d in dots]
    lane = iota((128, WIDTH), 1)
    products = jnp.where(
        lane == 0, high[0],
        jnp.where(lane == 1, high[1], jnp.where(lane == 2, dots[0] - high[0], jnp.where(lane == 3, dots[1] - high[1], 0.0))),
    ).astype(BF16)
    for s in range(reps):
        rows = slice(share * s, share * s + share)
        fin[s, 0:share, :] = share_out[rows, :]
        fin[s, share : 2 * share, :] = share_in[rows, :]
        fin[s, 2 * share :, :] = products[rows, :]
    for ro in range(1, reps):
        send(fin.at[lax.rem(rep + ro, reps)], fin_in.at[rep], y_send, y_recv, at_rep(ro))
    fin_in[rep] = fin[rep]

    wait(hx.at[pl.ds(0, reps - 1)], hx_recv)
    squares = None
    for s in range(reps):
        x = hx[s].astype(F32)
        part = jnp.sum(x * x, axis=1, keepdims=True)
        squares = part if s == 0 else squares + part
    root = jnp.sqrt(squares / features + EPSILON)

    wait(fin_in.at[pl.ds(0, reps - 1)], y_recv)
    inner = route = None
    for s in range(reps):
        cols = slice(WIDTH * s, WIDTH * s + WIDTH)
        x = hx[s].astype(F32)
        lo_ref[:, cols] = (x + fin_in[s, 0:share, :].astype(F32)).astype(BF16)
        scaled = gain_ref[:, cols] * fin_in[s, share : 2 * share, :].astype(F32)
        part = jnp.sum(scaled * x, axis=1, keepdims=True)
        inner = part if s == 0 else inner + part
        part = fin_in[s, 2 * share :, 0:128].astype(F32)
        route = part if s == 0 else route + part
    coefficient = inner / (features * root * root * root)
    for s in range(reps):
        cols = slice(WIDTH * s, WIDTH * s + WIDTH)
        scaled = gain_ref[:, cols] * fin_in[s, share : 2 * share, :].astype(F32)
        ig_ref[:, cols] = (scaled / root - hx[s].astype(F32) * coefficient).astype(BF16)
    rg_ref[...] = route[:, 0:2] + route[:, 2:4]

    wait(meta.at[1:NJ], tok_send.at[0])
    wait(tokh.at[1:NJ], tok_send.at[1])
    wait(tokg.at[1:NJ], tok_send.at[2])
    wait(hx.at[pl.ds(0, reps - 1)], hx_send)
    wait(zmain.at[0:240, :], zm_send)
    wait(zleft.at[0:240, :], zl_send)
    for c in range(CHUNKS):
        wait(gat.at[c, pl.ds(0, reps - 1)], c_send.at[c])
        wait(got.at[c, pl.ds(0, reps - 1)], e_send.at[c])
    wait(fmain.at[0:240, :], fm_send)
    wait(fleft.at[0:240, :], fl_send)
    wait(loc.at[1:4, 0:64, :], l_send.at[0])
    wait(loc.at[1:4, 64:80, :], l_send.at[1])
    wait(fin.at[pl.ds(0, reps - 1)], y_send)
    for copy in updates:
        copy.wait()


def body(hidden_in, norm_gain, route_ids, route_weights, w_gate, w_up, w_down, out_grad):
    reps = lax.axis_size("rep")
    units, features = w_gate.shape[1:]
    tokens = hidden_in.shape[0]
    vmem = pl.BlockSpec(memory_space=pltpu.VMEM)
    hbm = pl.BlockSpec(memory_space=pl.ANY)
    matrix = pltpu.VMEM((units, features), BF16)
    dma = pltpu.SemaphoreType.DMA
    rows = CHUNKS * ROWS
    scratch = [matrix] * 6 + [
        pltpu.VMEM((NJ, tokens, WIDTH), BF16),
        pltpu.VMEM((NJ, tokens, WIDTH), BF16),
        pltpu.VMEM((NJ, 8, tokens), F32),
        pltpu.VMEM((reps, tokens // reps, WIDTH), BF16),
        pltpu.VMEM((4 * ROWS, 2 * WIDTH), BF16),
        pltpu.VMEM((4 * ROWS, 128), BF16),
        pltpu.VMEM((4 * ROWS, 128), BF16),
        pltpu.VMEM((CHUNKS, reps, ROWS, 2 * WIDTH), BF16),
        pltpu.VMEM((CHUNKS, ROWS, features), BF16),
        pltpu.VMEM((CHUNKS, reps, ROWS, 2 * WIDTH), BF16),
        pltpu.VMEM((CHUNKS, reps, ROWS, 2 * WIDTH), BF16),
        pltpu.VMEM((4 * ROWS, 2 * WIDTH), BF16),
        pltpu.VMEM((4 * ROWS, 128), BF16),
        pltpu.VMEM((4 * ROWS, 2 * WIDTH), BF16),
        pltpu.VMEM((4 * ROWS, 128), BF16),
        pltpu.VMEM((NJ, 80, 2 * WIDTH), BF16),
        pltpu.VMEM((NJ, 80, 2 * WIDTH), BF16),
        pltpu.VMEM((reps, 3 * (tokens // reps), WIDTH), BF16),
        pltpu.VMEM((reps, 3 * (tokens // reps), WIDTH), BF16),
    ]
    scratch += [pltpu.VMEM((CHUNKS, ROWS, units), BF16)] * 3
    scratch += [pltpu.VMEM((units, rows), BF16)] * 3
    scratch += [
        dma((3,)), dma((3,)),
        dma((3,)), dma((3, NJ)),
        dma, dma,
        dma, dma((4,)),
        dma, dma,
        dma((CHUNKS,)), dma((CHUNKS,)),
        dma((CHUNKS,)), dma((CHUNKS,)),
        dma, dma, dma, dma,
        dma((2,)), dma((2, NJ)),
        dma, dma,
    ]
    update = jax.ShapeDtypeStruct((units, features), BF16)
    outs = pl.pallas_call(
        kernel,
        out_shape=(
            jax.ShapeDtypeStruct((tokens // reps, features), BF16),
            jax.ShapeDtypeStruct((tokens // reps, features), BF16),
            jax.ShapeDtypeStruct((tokens // reps, 2), F32),
            update, update, update,
        ),
        in_specs=[vmem] * 6 + [hbm] * 3,
        out_specs=(vmem, vmem, vmem, hbm, hbm, hbm),
        scratch_shapes=scratch,
        compiler_params=pltpu.CompilerParams(
            collective_id=0, has_side_effects=True, vmem_limit_bytes=48 * 1024 * 1024
        ),
        name="expert_layer",
    )(
        hidden_in, out_grad, route_ids.T, route_weights.T, route_weights, norm_gain[None, :],
        w_gate[0], w_up[0], w_down[0],
    )
    layer_out, input_grad, route_grad, gate_update, up_update, down_update = outs
    return layer_out, input_grad, route_grad, gate_update[None], up_update[None], down_update[None]


def solution(mesh):
    placed = (
        P("exp", "rep"),
        P(),
        P("exp", None),
        P("exp", None),
        P("exp", "rep", None),
        P("exp", "rep", None),
        P("exp", "rep", None),
        P("exp", "rep"),
    )
    return jax.shard_map(
        body,
        mesh=mesh,
        in_specs=placed,
        out_specs=(
            P(("exp", "rep"), None),
            P(("exp", "rep"), None),
            P(("exp", "rep"), None),
            P("exp", "rep", None),
            P("exp", "rep", None),
            P("exp", "rep", None),
        ),
        check_vma=False,
    )
```

```python
import functools

import jax
import jax.numpy as jnp
from jax import lax
from jax.experimental import pallas as pl
from jax.experimental.pallas import tpu as pltpu
from jax.sharding import PartitionSpec as P

MESH = pl.DeviceIdType.MESH
EPSILON = 1e-06
NZ = 16
NJ = 4
WIDTH = 256
CHUNKS = 5
ROWS = 64
F32 = jnp.float32
BF16 = jnp.bfloat16


OFFSETS = (1, 15, 2, 0, 14, 3, 13, 4, 12, 5, 11, 8, 6, 10, 7, 9)
HOME = OFFSETS.index(0)


def choose(index, values):
    out = jnp.full_like(index, values[0])
    for i in range(1, len(values)):
        out = jnp.where(index == i, values[i], out)
    return out


def z_offset(c, m):
    if isinstance(c, int):
        return OFFSETS[4 * c + m]
    return choose(c, OFFSETS[m::4])


def iota(shape, dim):
    return lax.broadcasted_iota(jnp.int32, shape, dim)


def dot(a, b, dims):
    return lax.dot_general(a, b, ((dims[:1], dims[1:]), ((), ())), preferred_element_type=F32)


def kernel(
    h_hbm, g_hbm, ids_ref, wrow_ref, gain_ref, wg_hbm, wu_hbm, wd_hbm,
    lo_ref, ig_ref, rg_ref, gu_out, uu_out, du_out,
    wg, wu, wd, gu, uu, du,
    tok, meta, pickm, wpick, hx, zmain, zleft, leftin, gat, nrm, par, got, fmain, fleft,
    fmain_in, fleft_in, loc, loc_in, fin, fin_in, hid, ggr, ugr, ht, ggt, ugt,
    w_sem, o_sem, own_sem, meta_send, meta_recv, tok_send, tok_recv, hx_send, hx_recv,
    zm_send, zm_recv, zl_send, zl_recv, c_send, c_recv, e_send, e_recv,
    fm_send, fm_recv, fl_send, fl_recv, l_send, l_recv, y_send, y_recv,
):
    reps = lax.axis_size("rep")
    features = reps * WIDTH
    share = h_hbm.shape[0] // reps
    rep = lax.axis_index("rep")
    exp = lax.axis_index("exp")
    z, j = exp // NJ, exp % NJ
    columns = reps // 2
    x, y = rep // 2, rep % 2

    def at_z(off):
        return {"exp": lax.rem(z + off, NZ) * NJ + j}

    def in_plane(d):
        return lax.rem(j // 2 + d // 2, 2) * 2 + lax.rem(j % 2 + d % 2, 2)

    def at_j(d):
        return {"exp": z * NJ + in_plane(d)}

    def rid(dx, dy):
        return lax.rem(x + columns + dx, columns) * 2 + lax.rem(y + dy, 2)

    def at(dx, dy):
        return {"rep": rid(dx, dy)}

    def send(src, dst, ssem, rsem, device):
        pltpu.make_async_remote_copy(
            src_ref=src, dst_ref=dst, send_sem=ssem, recv_sem=rsem, device_id=device, device_id_type=MESH
        ).start()

    def wait(ref, sem):
        pltpu.make_async_copy(ref, ref, sem).wait()

    own = [
        pltpu.make_async_copy(h_hbm, tok.at[0, :, 0:WIDTH], own_sem.at[0]),
        pltpu.make_async_copy(g_hbm, tok.at[0, :, WIDTH : 2 * WIDTH], own_sem.at[1]),
    ]
    weights = [
        pltpu.make_async_copy(wg_hbm, wg, w_sem.at[0]),
        pltpu.make_async_copy(wu_hbm, wu, w_sem.at[1]),
        pltpu.make_async_copy(wd_hbm, wd, w_sem.at[2]),
    ]
    for copy in own + weights:
        copy.start()

    barrier = pltpu.get_barrier_semaphore()

    def greet(off, carry):
        pl.semaphore_signal(barrier, inc=1, device_id=at_z(off), device_id_type=MESH)
        return carry

    for d in range(1, NJ):
        pl.semaphore_signal(barrier, inc=1, device_id=at_j(d), device_id_type=MESH)
    lax.fori_loop(1, NZ, greet, 0)
    for ro in range(1, reps):
        pl.semaphore_signal(barrier, inc=1, device_id=at(ro // 2, ro % 2), device_id_type=MESH)

    ids = ids_ref[...]
    expert_rows = iota((NZ * NJ, 128), 0)
    hits = [(expert_rows == ids[k : k + 1, :]).astype(F32) for k in range(2)]
    before = (iota((128, 128), 0) < iota((128, 128), 1)).astype(F32).astype(BF16)
    earlier = dot((hits[0] + hits[1]).astype(BF16), before, (1, 0))
    for k in range(2):
        number = jnp.sum(hits[k] * earlier, axis=0, keepdims=True)
        meta[0, k : k + 1, :] = ids[k : k + 1, :].astype(F32) * 8.0 + number
    meta[0, 2:4, :] = wrow_ref[...]
    meta[0, 4:8, :] = jnp.zeros((4, 128), F32)

    for copy in own:
        copy.wait()
    pl.semaphore_wait(barrier, NZ - 1 + NJ - 1 + reps - 1)

    for d in (2, 3, 1):
        send(meta.at[0], meta.at[d], meta_send, meta_recv, at_j(d))
    for half in range(2):
        rows = slice(64 * half, 64 * half + 64)
        send(tok.at[0, rows, :], tok.at[2, rows, :], tok_send, tok_recv.at[half], at_j(2))
    send(tok.at[0], tok.at[1], tok_send, tok_recv.at[2], at_j(1))

    def code_of(place, number):
        plane = (z + choose(place, OFFSETS)) & (NZ - 1)
        return ((plane * NJ + j) * 8 + number).astype(F32)

    def pick(code, block, at_rows):
        weight = None
        for d in range(NJ):
            mine = jnp.where(block == d, code, -1.0)
            one = [mine == meta[d, k : k + 1, :] for k in range(2)]
            pickm[at_rows, 128 * d : 128 * d + 128] = (one[0] | one[1]).astype(F32).astype(BF16)
            w = jnp.sum(
                jnp.where(one[0], meta[d, 2:3, :], 0.0) + jnp.where(one[1], meta[d, 3:4, :], 0.0), axis=1, keepdims=True
            )
            weight = w if d == 0 else weight + w
        wpick[at_rows, :] = weight

    wait(meta.at[1:NJ], meta_recv)
    r = iota((ROWS, 1), 0)
    for c in range(4):
        pick(code_of(4 * c + (r >> 4), r & 3), (r >> 2) & 3, slice(c * ROWS, (c + 1) * ROWS))
    pick(code_of(r >> 2, 4), r & 3, slice(4 * ROWS, 5 * ROWS))

    for half in range(2):
        rows = slice(64 * half, 64 * half + 64)
        wait(tok.at[2, rows, :], tok_recv.at[half])
        send(tok.at[2, rows, :], tok.at[3, rows, :], tok_send, tok_recv.at[3 + half], at_j(1))
    wait(tok.at[1], tok_recv.at[2])
    for half in range(2):
        wait(tok.at[3, 64 * half : 64 * half + 64, :], tok_recv.at[3 + half])
    tokens = tok[...].reshape(NJ * tok.shape[1], 2 * WIDTH)

    def rows_of(at_rows):
        rows = dot(pickm[at_rows, :], tokens, (1, 0))
        return rows[:, 0:WIDTH].astype(BF16), (wpick[at_rows, :] * rows[:, WIDTH:]).astype(BF16)

    for c in range(4):
        rows_h, rows_g = rows_of(slice(c * ROWS, (c + 1) * ROWS))
        zmain[c * ROWS : (c + 1) * ROWS, 0:WIDTH] = rows_h
        zmain[c * ROWS : (c + 1) * ROWS, WIDTH : 2 * WIDTH] = rows_g
        for m in range(4):
            if 4 * c + m == HOME:
                gat[0, rep, 48:64, :] = zmain[48:64, :]
                continue
            send(
                zmain.at[c * ROWS + 16 * m : c * ROWS + 16 * m + 16, :],
                gat.at[c, rep, 16 * m : 16 * m + 16, :],
                zm_send, zm_recv.at[c], at_z(z_offset(c, m)),
            )

    def spread(part, to_blocks):
        r, t = iota((ROWS, 4 * ROWS), 0), iota((ROWS, 4 * ROWS), 1)
        place, block = (r & 15, r >> 4) if to_blocks else (r >> 2, r & 3)
        return (t == 16 * place + 4 * part + block).astype(F32).astype(BF16)

    def to_tiles(rows):
        tiles = None
        for part in range(4):
            one = dot(spread(part, False), rows[:, 128 * part : 128 * part + 128], (0, 0))
            tiles = one if part == 0 else tiles + one
        return tiles.astype(BF16)

    rows_h, rows_g = rows_of(slice(4 * ROWS, 5 * ROWS))
    zleft[...] = to_tiles(jnp.concatenate([rows_h, rows_g], axis=1))
    leftin[48:64, :] = zleft[48:64, :]

    def send_left(src, dst, ssem, rsem, sign):
        for place in range(16):
            if place == HOME:
                continue
            off = OFFSETS[place]
            rows = slice(16 * place, 16 * place + 16)
            send(src.at[rows, :], dst.at[rows, :], ssem, rsem, at_z(off if sign > 0 else NZ - off))

    send_left(zleft, leftin, zl_send, zl_recv, 1)

    for ro in range(1, reps):
        to = rid(ro // 2, ro % 2)
        rows = pl.ds(pl.multiple_of(to * share, 16), share)
        send(tok.at[0, rows, 0:WIDTH], hx.at[rep], hx_send, hx_recv, at(ro // 2, ro % 2))
    hx[rep] = tok[0, pl.ds(pl.multiple_of(rep * share, 16), share), 0:WIDTH]

    for copy in weights:
        copy.wait()

    low, high = slice(0, ROWS // 2), slice(ROWS // 2, ROWS)

    def gather(c):
        mine = gat.at[c, rep]
        send(mine, mine, c_send.at[c], c_recv.at[c, 0], at(0, 1))
        send(mine, mine, c_send.at[c], c_recv.at[c, 1], at(1, 0))
        send(mine, mine, c_send.at[c], c_recv.at[c, 2], at(-1, 0))

    def stage_0(c):
        @pl.when(c == 0)
        def _():
            wait(gat.at[c, rep, 0:48, :], zm_recv.at[0])
            gather(c)

        @pl.when((c > 0) & (c < 4))
        def _():
            wait(gat.at[c, rep], zm_recv.at[c])
            gather(c)

        @pl.when(c == 4)
        def _():
            wait(leftin.at[0:240, :], zl_recv)
            for part in range(4):
                cols = slice(128 * part, 128 * part + 128)
                gat[c, rep, :, cols] = dot(spread(part, False), leftin[...], (1, 0)).astype(BF16)
            gather(c)

    def stage_1(c):
        other, left, right = gat.at[c, rid(0, 1)], gat.at[c, rid(-1, 0)], gat.at[c, rid(1, 0)]
        wait(other, c_recv.at[c, 0])
        send(other, other, c_send.at[c], c_recv.at[c, 3], at(1, 0))
        send(other, other, c_send.at[c], c_recv.at[c, 4], at(-1, 0))
        wait(left, c_recv.at[c, 1])
        send(left.at[low, :], left.at[low, :], c_send.at[c], c_recv.at[c, 5], at(1, 0))
        wait(right, c_recv.at[c, 2])
        send(right.at[high, :], right.at[high, :], c_send.at[c], c_recv.at[c, 6], at(-1, 0))

    def stage_2(c):
        far = gat.at[c, rid(2, 0)]
        wait(far.at[low, :], c_recv.at[c, 5])
        wait(far.at[high, :], c_recv.at[c, 6])
        send(far, far, c_send.at[c], c_recv.at[c, 7], at(0, 1))

    def stage_3(c):
        wait(gat.at[c, rid(-1, 1)], c_recv.at[c, 3])
        wait(gat.at[c, rid(1, 1)], c_recv.at[c, 4])
        wait(gat.at[c, rid(2, 1)], c_recv.at[c, 7])
        squares = None
        for s in range(reps):
            v = gat[c, s, :, 0:WIDTH].astype(F32)
            part = jnp.sum(v * v, axis=1, keepdims=True)
            squares = part if s == 0 else squares + part
        scale = 1.0 / jnp.sqrt(squares / features + EPSILON)
        hidden_grad = None
        for s in range(reps):
            cols = slice(WIDTH * s, WIDTH * s + WIDTH)
            v = gat[c, s, :, 0:WIDTH].astype(F32)
            nrm[c, :, cols] = (v * gain_ref[:, cols] * scale).astype(BF16)
            part = dot(gat[c, s, :, WIDTH : 2 * WIDTH], wd[:, cols], (1, 1))
            hidden_grad = part if s == 0 else hidden_grad + part
        gate_pre = dot(nrm[c], wg[...], (1, 1))
        up_pre = dot(nrm[c], wu[...], (1, 1))
        sig = jax.nn.sigmoid(gate_pre)
        activated = gate_pre * sig
        hidden = (activated * up_pre).astype(BF16)
        gate_grad = (hidden_grad * up_pre * sig * (1.0 + gate_pre * (1.0 - sig))).astype(BF16)
        up_grad = (hidden_grad * activated).astype(BF16)
        hid[c], ggr[c], ugr[c] = hidden, gate_grad, up_grad
        for s in range(reps):
            cols = slice(WIDTH * s, WIDTH * s + WIDTH)
            par[c, s, :, 0:WIDTH] = dot(hidden, wd[:, cols], (1, 0)).astype(BF16)
            par[c, s, :, WIDTH : 2 * WIDTH] = (
                dot(gate_grad, wg[:, cols], (1, 0)) + dot(up_grad, wu[:, cols], (1, 0))
            ).astype(BF16)
        send(par.at[c, rid(2, 1)], got.at[c, 0], e_send.at[c], e_recv.at[c, 0], at(0, 1))
        send(par.at[c, rid(1, 1)], got.at[c, 1], e_send.at[c], e_recv.at[c, 1], at(1, 0))
        send(par.at[c, rid(-1, 1)], got.at[c, 2], e_send.at[c], e_recv.at[c, 2], at(-1, 0))

    def stage_4(c):
        far, other = rid(2, 0), rid(0, 1)
        wait(got.at[c, 0], e_recv.at[c, 0])
        par[c, far] = (par[c, far].astype(F32) + got[c, 0].astype(F32)).astype(BF16)
        send(par.at[c, far, low, :], got.at[c, 3, low, :], e_send.at[c], e_recv.at[c, 3], at(1, 0))
        send(par.at[c, far, high, :], got.at[c, 3, high, :], e_send.at[c], e_recv.at[c, 7], at(-1, 0))
        wait(got.at[c, 1], e_recv.at[c, 1])
        wait(got.at[c, 2], e_recv.at[c, 2])
        par[c, other] = (
            par[c, other].astype(F32) + got[c, 1].astype(F32) + got[c, 2].astype(F32)
        ).astype(BF16)
        send(par.at[c, other], got.at[c, 6], e_send.at[c], e_recv.at[c, 6], at(0, 1))

    def stage_5(c):
        right, left = rid(1, 0), rid(-1, 0)
        wait(got.at[c, 3, low, :], e_recv.at[c, 3])
        par[c, right, low, :] = (par[c, right, low, :].astype(F32) + got[c, 3, low, :].astype(F32)).astype(BF16)
        send(par.at[c, right], got.at[c, 4], e_send.at[c], e_recv.at[c, 4], at(1, 0))
        wait(got.at[c, 3, high, :], e_recv.at[c, 7])
        par[c, left, high, :] = (par[c, left, high, :].astype(F32) + got[c, 3, high, :].astype(F32)).astype(BF16)
        send(par.at[c, left], got.at[c, 5], e_send.at[c], e_recv.at[c, 5], at(-1, 0))

    def stage_6(c):
        total = par[c, rep].astype(F32)
        for k in (6, 4, 5):
            wait(got.at[c, k], e_recv.at[c, k])
            total = total + got[c, k].astype(F32)
        total = total.astype(BF16)

        @pl.when(c < 4)
        def _():
            start = pl.multiple_of(c * ROWS, ROWS)
            fmain[pl.ds(start, ROWS), :] = total
            for m in range(4):
                rows = pl.ds(pl.multiple_of(start + 16 * m, 16), 16)

                def far(rows=rows, m=m):
                    send(fmain.at[rows, :], fmain_in.at[rows, :], fm_send, fm_recv.at[c], at_z(NZ - z_offset(c, m)))

                if m == HOME:
                    pl.when(c > 0)(far)

                    @pl.when(c == 0)
                    def _():
                        fmain_in[48:64, :] = total[48:64, :]
                else:
                    far()

        @pl.when(c == 4)
        def _():
            tiles = to_tiles(total)
            fleft[...] = tiles
            fleft_in[48:64, :] = tiles[48:64, :]
            send_left(fleft, fleft_in, fl_send, fl_recv, -1)

    def to_blocks(c):
        rows = pl.ds(pl.multiple_of(16 * c, 16), 16)
        for d in range(1, NJ):
            send(loc.at[d, rows, :], loc_in.at[d, rows, :], l_send, l_recv, at_j(d))

    def stage_7(c):
        @pl.when(c < 4)
        def _():
            @pl.when(c == 0)
            def _():
                wait(fmain_in.at[0:48, :], fm_recv.at[0])

            @pl.when(c > 0)
            def _():
                wait(fmain_in.at[0:64, :], fm_recv.at[c])

            r, t = iota((ROWS, ROWS), 0), iota((ROWS, ROWS), 1)
            regroup = (t == 16 * ((r >> 2) & 3) + 4 * (r >> 4) + (r & 3)).astype(F32).astype(BF16)
            back = fmain_in[pl.ds(pl.multiple_of(c * ROWS, ROWS), ROWS), :]
            main = dot(regroup, back, (1, 0)).astype(BF16)
            rows = pl.ds(pl.multiple_of(16 * c, 16), 16)
            loc_in[0, rows, :] = main[0:16, :]
            for d in range(1, NJ):
                loc[d, rows, :] = main[16 * d : 16 * d + 16, :]
            to_blocks(c)

        @pl.when(c == 4)
        def _():
            wait(fleft_in.at[0:240, :], fl_recv)
            for part in range(4):
                cols = slice(128 * part, 128 * part + 128)
                fifth = dot(spread(part, True), fleft_in[...], (1, 0)).astype(BF16)
                loc_in[0, 64:80, cols] = fifth[0:16, :]
                for d in range(1, NJ):
                    loc[d, 64:80, cols] = fifth[16 * d : 16 * d + 16, :]
            to_blocks(c)

    def turned(ref):
        return jnp.transpose(ref[...].reshape(CHUNKS * ROWS, ref.shape[2]).astype(F32)).astype(BF16)

    def update(s):
        cols = pl.ds(pl.multiple_of(s * WIDTH, WIDTH), WIDTH)
        rows_n = nrm[:, :, cols].reshape(CHUNKS * ROWS, WIDTH)
        rows_g = gat[:, s, :, WIDTH : 2 * WIDTH].reshape(CHUNKS * ROWS, WIDTH)
        gu[:, cols] = dot(ggt[...], rows_n, (1, 0)).astype(BF16)
        uu[:, cols] = dot(ugt[...], rows_n, (1, 0)).astype(BF16)
        du[:, cols] = dot(ht[...], rows_g, (1, 0)).astype(BF16)

    stages = (
        (9, stage_7), (6, stage_6), (5, stage_5), (4, stage_4), (3, stage_3), (2, stage_2), (1, stage_1), (0, stage_0)
    )
    first_free = CHUNKS + 3
    ticks = CHUNKS + stages[0][0]
    per_tick = 2

    def tick(t, carry):
        for lag, stage in stages:
            pl.when((t >= lag) & (t - lag < CHUNKS))(functools.partial(stage, t - lag))

        @pl.when(t == first_free)
        def _():
            ht[...], ggt[...], ugt[...] = turned(hid), turned(ggr), turned(ugr)

        @pl.when((t >= first_free) & (t < first_free + reps // per_tick))
        def _():
            for s in range(per_tick):
                update((t - first_free) * per_tick + s)

        return carry

    lax.fori_loop(0, ticks, tick, 0)

    updates = [
        pltpu.make_async_copy(gu, gu_out, o_sem.at[0]),
        pltpu.make_async_copy(uu, uu_out, o_sem.at[1]),
        pltpu.make_async_copy(du, du_out, o_sem.at[2]),
    ]
    for copy in updates:
        copy.start()

    r = iota((80, 1), 0)
    place = jnp.where(r < 64, r >> 2, r - 64)
    number = jnp.where(r < 64, r & 3, 4)
    plane = (z + choose(place, OFFSETS)) & (NZ - 1)
    codes = [((plane * NJ + in_plane(d)) * 8 + number).astype(F32) for d in range(NJ)]
    ones = [
        jnp.concatenate([(code == meta[0, k : k + 1, :]).astype(F32).astype(BF16) for code in codes], axis=0)
        for k in range(2)
    ]
    grad = tok[0, :, WIDTH:].astype(F32)
    diagonal = iota((128, 128), 0) == iota((128, 128), 1)
    w = [jnp.sum(jnp.where(diagonal, meta[0, 2 + k : 3 + k, :], 0.0), axis=1, keepdims=True) for k in range(2)]
    wait(hx.at[pl.ds(0, reps - 1)], hx_recv)
    squares = None
    for s in range(reps):
        v = hx[s].astype(F32)
        part = jnp.sum(v * v, axis=1, keepdims=True)
        squares = part if s == 0 else squares + part
    root = jnp.sqrt(squares / features + EPSILON)

    wait(loc_in.at[1:NJ], l_recv)
    rows = loc_in[...].reshape(NJ * 80, 2 * WIDTH)
    picked = [dot(one, rows, (0, 0)) for one in ones]
    out_rows = [p[:, 0:WIDTH] for p in picked]
    share_out = (w[0] * out_rows[0] + w[1] * out_rows[1]).astype(BF16)
    share_in = (picked[0][:, WIDTH:] + picked[1][:, WIDTH:]).astype(BF16)
    dots = [jnp.sum(p * grad, axis=1, keepdims=True) for p in out_rows]
    heads = [d.astype(BF16).astype(F32) for d in dots]
    lane = iota((128, WIDTH), 1)
    products = jnp.where(
        lane == 0, heads[0],
        jnp.where(lane == 1, heads[1], jnp.where(lane == 2, dots[0] - heads[0], jnp.where(lane == 3, dots[1] - heads[1], 0.0))),
    ).astype(BF16)
    for s in range(reps):
        rows = slice(share * s, share * s + share)
        fin[s, 0:share, :] = share_out[rows, :]
        fin[s, share : 2 * share, :] = share_in[rows, :]
        fin[s, 2 * share :, :] = products[rows, :]
    for ro in range(1, reps):
        send(fin.at[rid(ro // 2, ro % 2)], fin_in.at[rep], y_send, y_recv, at(ro // 2, ro % 2))
    fin_in[rep] = fin[rep]

    wait(fin_in.at[pl.ds(0, reps - 1)], y_recv)
    inner = route = None
    for s in range(reps):
        cols = slice(WIDTH * s, WIDTH * s + WIDTH)
        v = hx[s].astype(F32)
        lo_ref[:, cols] = (v + fin_in[s, 0:share, :].astype(F32)).astype(BF16)
        scaled = gain_ref[:, cols] * fin_in[s, share : 2 * share, :].astype(F32)
        part = jnp.sum(scaled * v, axis=1, keepdims=True)
        inner = part if s == 0 else inner + part
        part = fin_in[s, 2 * share :, 0:128].astype(F32)
        route = part if s == 0 else route + part
    coefficient = inner / (features * root * root * root)
    for s in range(reps):
        cols = slice(WIDTH * s, WIDTH * s + WIDTH)
        scaled = gain_ref[:, cols] * fin_in[s, share : 2 * share, :].astype(F32)
        ig_ref[:, cols] = (scaled / root - hx[s].astype(F32) * coefficient).astype(BF16)
    diagonal = iota((share, share), 0) == iota((share, share), 1)
    for k in range(2):
        column = route[:, k : k + 1] + route[:, 2 + k : 3 + k]
        rg_ref[k : k + 1, :] = jnp.sum(jnp.where(diagonal, column, 0.0), axis=0, keepdims=True)

    wait(meta.at[1:NJ], meta_send)
    wait(tok.at[1:NJ], tok_send)
    wait(hx.at[pl.ds(0, reps - 1)], hx_send)
    wait(zmain.at[0:240, :], zm_send)
    wait(zleft.at[0:240, :], zl_send)
    for c in range(CHUNKS):
        wait(gat.at[c, pl.ds(0, 7)], c_send.at[c])
        wait(got.at[c], e_send.at[c])
    wait(fmain.at[0:240, :], fm_send)
    wait(fleft.at[0:240, :], fl_send)
    wait(loc.at[1:NJ], l_send)
    wait(fin.at[pl.ds(0, reps - 1)], y_send)
    for copy in updates:
        copy.wait()


def hand_out(*refs):
    n = len(refs) // 2
    copies = [pltpu.make_async_copy(refs[i], refs[n + i], refs[2 * n].at[i]) for i in range(n)]
    for copy in copies:
        copy.start()
    for copy in copies:
        copy.wait()


def body(hidden_in, norm_gain, route_ids, route_weights, w_gate, w_up, w_down, out_grad):
    reps = lax.axis_size("rep")
    units, features = w_gate.shape[1:]
    tokens = hidden_in.shape[0]
    share = tokens // reps
    vmem = pl.BlockSpec(memory_space=pltpu.VMEM)
    hbm = pl.BlockSpec(memory_space=pltpu.HBM)
    anywhere = pl.BlockSpec(memory_space=pl.ANY)
    matrix = pltpu.VMEM((units, features), BF16)
    dma = pltpu.SemaphoreType.DMA
    rows = CHUNKS * ROWS
    scratch = [matrix] * 6 + [
        pltpu.VMEM((NJ, tokens, 2 * WIDTH), BF16),
        pltpu.VMEM((NJ, 8, tokens), F32),
        pltpu.VMEM((rows, NJ * tokens), BF16),
        pltpu.VMEM((rows, 1), F32),
        pltpu.VMEM((reps, share, WIDTH), BF16),
        pltpu.VMEM((4 * ROWS, 2 * WIDTH), BF16),
        pltpu.VMEM((4 * ROWS, 128), BF16),
        pltpu.VMEM((4 * ROWS, 128), BF16),
        pltpu.VMEM((CHUNKS, reps, ROWS, 2 * WIDTH), BF16),
        pltpu.VMEM((CHUNKS, ROWS, features), BF16),
        pltpu.VMEM((CHUNKS, reps, ROWS, 2 * WIDTH), BF16),
        pltpu.VMEM((CHUNKS, 7, ROWS, 2 * WIDTH), BF16),
        pltpu.VMEM((4 * ROWS, 2 * WIDTH), BF16),
        pltpu.VMEM((4 * ROWS, 128), BF16),
        pltpu.VMEM((4 * ROWS, 2 * WIDTH), BF16),
        pltpu.VMEM((4 * ROWS, 128), BF16),
        pltpu.VMEM((NJ, 80, 2 * WIDTH), BF16),
        pltpu.VMEM((NJ, 80, 2 * WIDTH), BF16),
        pltpu.VMEM((reps, 3 * share, WIDTH), BF16),
        pltpu.VMEM((reps, 3 * share, WIDTH), BF16),
    ]
    scratch += [pltpu.VMEM((CHUNKS, ROWS, units), BF16)] * 3
    scratch += [pltpu.VMEM((units, rows), BF16)] * 3
    scratch += [
        dma((3,)), dma((3,)), dma((2,)),
        dma, dma, dma, dma((5,)),
        dma, dma,
        dma, dma((4,)),
        dma, dma,
        dma((CHUNKS,)), dma((CHUNKS, 8)),
        dma((CHUNKS,)), dma((CHUNKS, 8)),
        dma, dma((4,)), dma, dma,
        dma, dma,
        dma, dma,
    ]
    update = jax.ShapeDtypeStruct((units, features), BF16)
    kinds = (
        jax.ShapeDtypeStruct((share, features), BF16),
        jax.ShapeDtypeStruct((share, features), BF16),
        jax.ShapeDtypeStruct((2, share), F32),
        update, update, update,
    )
    outs = pl.pallas_call(
        kernel,
        out_shape=kinds,
        in_specs=[hbm] * 2 + [vmem] * 3 + [hbm] * 3,
        out_specs=(vmem, vmem, vmem, anywhere, anywhere, anywhere),
        scratch_shapes=scratch,
        compiler_params=pltpu.CompilerParams(
            collective_id=0, has_side_effects=True, vmem_limit_bytes=62 * 1024 * 1024
        ),
        name="expert_layer",
    )(
        hidden_in, out_grad, route_ids.T, route_weights.T, norm_gain[None, :], w_gate[0], w_up[0], w_down[0]
    )
    outs = pl.pallas_call(
        hand_out,
        out_shape=kinds,
        in_specs=[vmem] * 6,
        out_specs=(anywhere,) * 6,
        scratch_shapes=[dma((6,))],
        name="results",
    )(*outs)
    layer_out, input_grad, route_grad, gate_update, up_update, down_update = outs
    return layer_out, input_grad, route_grad.T, gate_update[None], up_update[None], down_update[None]


def solution(mesh):
    placed = (
        P("exp", "rep"),
        P(),
        P("exp", None),
        P("exp", None),
        P("exp", "rep", None),
        P("exp", "rep", None),
        P("exp", "rep", None),
        P("exp", "rep"),
    )
    return jax.shard_map(
        body,
        mesh=mesh,
        in_specs=placed,
        out_specs=(
            P(("exp", "rep"), None),
            P(("exp", "rep"), None),
            P(("exp", "rep"), None),
            P("exp", "rep", None),
            P("exp", "rep", None),
            P("exp", "rep", None),
        ),
        check_vma=False,
    )
```

```python
import functools

import jax
import jax.numpy as jnp
from jax import lax
from jax.experimental import pallas as pl
from jax.experimental.pallas import tpu as pltpu
from jax.sharding import PartitionSpec as P

MESH = pl.DeviceIdType.MESH
EPSILON = 1e-06
NZ = 16
NJ = 4
WIDTH = 256
CHUNKS = 5
FIFTH = 3
ROWS = 64
F32 = jnp.float32
BF16 = jnp.bfloat16


OFFSETS = ((1, 15, 2, 0), (12, 5, 11, 8), (6, 10, 7, 9), None, (14, 3, 13, 4))
MAIN = tuple(c for c in range(CHUNKS) if c != FIFTH)
ALL = sum((OFFSETS[c] for c in MAIN), ())
HOME = ALL.index(0)


def choose(index, values):
    out = jnp.full_like(index, values[0])
    for i in range(1, len(values)):
        out = jnp.where(index == i, values[i], out)
    return out


def z_offset(c, m):
    if isinstance(c, int):
        return OFFSETS[c][m]
    return choose(c, [OFFSETS[i][m] if i != FIFTH else 0 for i in range(CHUNKS)])


def iota(shape, dim):
    return lax.broadcasted_iota(jnp.int32, shape, dim)


def dot(a, b, dims):
    return lax.dot_general(a, b, ((dims[:1], dims[1:]), ((), ())), preferred_element_type=F32)


def kernel(
    h_hbm, g_hbm, ids_ref, wrow_ref, gain_ref, wg_hbm, wu_hbm, wd_hbm,
    lo_ref, ig_ref, rg_ref, gu_out, uu_out, du_out,
    wg, wu, wd, gu, uu, du,
    tok, meta, hx, zout, zin, gat, nrm, par, got, fout, fback, loc, rows_in, fin, fin_in,
    hid, ggr, ugr, ht, ggt, ugt,
    w_sem, o_sem, own_sem, meta_send, meta_recv, tok_send, tok_recv, hx_send, hx_recv,
    z_send, z_recv, c_send, c_recv, e_send, e_recv, f_send, f_recv, l_send, l_recv, y_send, y_recv,
):
    reps = lax.axis_size("rep")
    features = reps * WIDTH
    share = h_hbm.shape[0] // reps
    rep = lax.axis_index("rep")
    exp = lax.axis_index("exp")
    z, j = exp // NJ, exp % NJ
    columns = reps // 2
    x, y = rep // 2, rep % 2

    def in_plane(d):
        return lax.rem(j // 2 + d // 2, 2) * 2 + lax.rem(j % 2 + d % 2, 2)

    def at_place(off, d):
        return {"exp": lax.rem(z + off, NZ) * NJ + in_plane(d)}

    def rid(dx, dy):
        return lax.rem(x + columns + dx, columns) * 2 + lax.rem(y + dy, 2)

    def at(dx, dy):
        return {"rep": rid(dx, dy)}

    def send(src, dst, ssem, rsem, device):
        pltpu.make_async_remote_copy(
            src_ref=src, dst_ref=dst, send_sem=ssem, recv_sem=rsem, device_id=device, device_id_type=MESH
        ).start()

    def wait(ref, sem):
        pltpu.make_async_copy(ref, ref, sem).wait()

    own = [
        pltpu.make_async_copy(h_hbm, tok.at[0, :, 0:WIDTH], own_sem.at[0]),
        pltpu.make_async_copy(g_hbm, tok.at[0, :, WIDTH : 2 * WIDTH], own_sem.at[1]),
    ]
    weights = [
        pltpu.make_async_copy(wg_hbm, wg, w_sem.at[0]),
        pltpu.make_async_copy(wu_hbm, wu, w_sem.at[1]),
        pltpu.make_async_copy(wd_hbm, wd, w_sem.at[2]),
    ]
    for copy in own + weights:
        copy.start()

    barrier = pltpu.get_barrier_semaphore()

    def greet(off, carry):
        pl.semaphore_signal(barrier, inc=1, device_id={"exp": lax.rem(exp + off, NZ * NJ)}, device_id_type=MESH)
        return carry

    lax.fori_loop(1, NZ * NJ, greet, 0)
    for ro in range(1, reps):
        pl.semaphore_signal(barrier, inc=1, device_id=at(ro // 2, ro % 2), device_id_type=MESH)

    ids = ids_ref[...]
    expert_rows = iota((NZ * NJ, 128), 0)
    hits = [(expert_rows == ids[k : k + 1, :]).astype(F32) for k in range(2)]
    before = (iota((128, 128), 0) < iota((128, 128), 1)).astype(F32).astype(BF16)
    earlier = dot((hits[0] + hits[1]).astype(BF16), before, (1, 0))
    for k in range(2):
        number = jnp.sum(hits[k] * earlier, axis=0, keepdims=True)
        meta[0, k : k + 1, :] = ids[k : k + 1, :].astype(F32) * 8.0 + number
    meta[0, 2:4, :] = wrow_ref[...]
    meta[0, 4:8, :] = jnp.zeros((4, 128), F32)

    for copy in own:
        copy.wait()

    def code_of(off, place, number):
        plane = (z + off) & (NZ - 1)
        return ((plane * NJ + choose(place, [in_plane(d) for d in range(NJ)])) * 8 + number).astype(F32)

    r = iota((4 * ROWS, 1), 0)
    part_of = (r >> 2) & 3
    blocks = jnp.concatenate([tok[0, :, 128 * f : 128 * f + 128] for f in range(4)], axis=0)

    def pick(code, d):
        one = [code == meta[d, k : k + 1, :] for k in range(2)]
        w = jnp.where(one[0], meta[d, 2:3, :], 0.0) + jnp.where(one[1], meta[d, 3:4, :], 0.0)
        return (one[0] | one[1]).astype(F32), jnp.sum(w, axis=1, keepdims=True)

    def build(c):
        hit, weight = pick(code_of(choose(r >> 6, OFFSETS[c]), (r >> 4) & 3, r & 3), 0)
        masks = jnp.concatenate([jnp.where(part_of == f, hit, 0.0) for f in range(4)], axis=1).astype(BF16)
        tiles = dot(masks, blocks, (1, 0))
        zout[c] = jnp.where(part_of >= 2, weight * tiles, tiles).astype(BF16)

    build(0)
    pl.semaphore_wait(barrier, NZ * NJ - 1 + reps - 1)

    def send_tiles(src, dst, ssem, rsem, c, sign):
        for m in range(4):
            off = z_offset(c, m)
            off = off if sign > 0 else NZ - off
            for d in range(NJ):
                rows = slice(64 * m + 16 * d, 64 * m + 16 * d + 16)

                def far(rows=rows, d=d, off=off):
                    send(src.at[c, rows, :], dst.at[c, rows, :], ssem.at[c], rsem.at[c], at_place(off, d))

                if m == HOME and d == 0:
                    if not isinstance(c, int):
                        pl.when(c > 0)(far)
                    elif c > 0:
                        far()
                else:
                    far()

    def send_fifth(src, dst, ssem, rsem, sign):
        for place, off in enumerate(ALL):
            if place != HOME:
                rows = slice(16 * place, 16 * place + 16)
                to = at_place(off if sign > 0 else NZ - off, 0)
                send(src.at[FIFTH, rows, :], dst.at[FIFTH, rows, :], ssem.at[FIFTH], rsem.at[FIFTH], to)

    own_tile = slice(64 * HOME, 64 * HOME + 16)
    own_fifth = slice(16 * HOME, 16 * HOME + 16)
    send_tiles(zout, zin, z_send, z_recv, 0, 1)
    zin[0, own_tile, :] = zout[0, own_tile, :]

    for d in (2, 3, 1):
        send(meta.at[0], meta.at[d], meta_send, meta_recv, at_place(0, d))
    send(tok.at[0], tok.at[2], tok_send, tok_recv.at[1], at_place(0, 2))
    send(tok.at[0], tok.at[1], tok_send, tok_recv.at[0], at_place(0, 1))
    for c in MAIN[1:]:
        build(c)
        send_tiles(zout, zin, z_send, z_recv, c, 1)

    def hand_on():
        wait(tok.at[2], tok_recv.at[1])
        send(tok.at[2], tok.at[3], tok_send, tok_recv.at[2], at_place(0, 1))

    def spread(part, to_blocks):
        r, t = iota((ROWS, 4 * ROWS), 0), iota((ROWS, 4 * ROWS), 1)
        tile, d = (r & 15, r >> 4) if to_blocks else (r >> 2, r & 3)
        return (t == 16 * tile + 4 * part + d).astype(F32).astype(BF16)

    def to_tiles(rows):
        tiles = None
        for part in range(4):
            one = dot(spread(part, False), rows[:, 128 * part : 128 * part + 128], (0, 0))
            tiles = one if part == 0 else tiles + one
        return tiles.astype(BF16)

    def send_fifth_rows():
        wait(meta.at[1:NJ], meta_recv)
        wait(tok.at[1], tok_recv.at[0])
        wait(tok.at[3], tok_recv.at[2])
        r = iota((ROWS, 1), 0)
        code = code_of(choose(r >> 2, ALL), jnp.zeros_like(r), jnp.full_like(r, 4))
        rows = weight = None
        for d in range(NJ):
            hit, w = pick(jnp.where((r & 3) == d, code, -1.0), d)
            one = dot(hit.astype(BF16), tok[d], (1, 0))
            rows = one if d == 0 else rows + one
            weight = w if d == 0 else weight + w
        lanes = iota((1, 2 * WIDTH), 1)
        tiles = to_tiles(jnp.where(lanes < WIDTH, rows, weight * rows).astype(BF16))
        zout[FIFTH] = tiles
        zin[FIFTH, own_fifth, :] = tiles[own_fifth, :]
        send_fifth(zout, zin, z_send, z_recv, 1)

    for ro in range(1, reps):
        to = rid(ro // 2, ro % 2)
        rows = pl.ds(pl.multiple_of(to * share, 16), share)
        send(tok.at[0, rows, 0:WIDTH], hx.at[rep], hx_send, hx_recv, at(ro // 2, ro % 2))
    hx[rep] = tok[0, pl.ds(pl.multiple_of(rep * share, 16), share), 0:WIDTH]

    for copy in weights:
        copy.wait()

    low, high = slice(0, ROWS // 2), slice(ROWS // 2, ROWS)

    def gather(c):
        mine = gat.at[c, rep]
        send(mine, mine, c_send.at[c], c_recv.at[c, 0], at(0, 1))
        send(mine, mine, c_send.at[c], c_recv.at[c, 1], at(1, 0))
        send(mine, mine, c_send.at[c], c_recv.at[c, 2], at(-1, 0))

    def wait_tiles(ref, sem, c):
        fewer = (c == 0) | (c == FIFTH)

        @pl.when(fewer)
        def _():
            wait(ref.at[c, 0:240, :], sem.at[c])

        @pl.when(jnp.logical_not(fewer))
        def _():
            wait(ref.at[c], sem.at[c])

    def stage_0(c):
        wait_tiles(zin, z_recv, c)
        tiles = zin[c]
        for part in range(4):
            cols = slice(128 * part, 128 * part + 128)
            gat[c, rep, :, cols] = dot(spread(part, False), tiles, (1, 0)).astype(BF16)
        gather(c)

    def stage_1(c):
        other, left, right = gat.at[c, rid(0, 1)], gat.at[c, rid(-1, 0)], gat.at[c, rid(1, 0)]
        wait(other, c_recv.at[c, 0])
        send(other, other, c_send.at[c], c_recv.at[c, 3], at(1, 0))
        send(other, other, c_send.at[c], c_recv.at[c, 4], at(-1, 0))
        wait(left, c_recv.at[c, 1])
        send(left.at[low, :], left.at[low, :], c_send.at[c], c_recv.at[c, 5], at(1, 0))
        wait(right, c_recv.at[c, 2])
        send(right.at[high, :], right.at[high, :], c_send.at[c], c_recv.at[c, 6], at(-1, 0))

    def stage_2(c):
        far = gat.at[c, rid(2, 0)]
        wait(far.at[low, :], c_recv.at[c, 5])
        wait(far.at[high, :], c_recv.at[c, 6])
        send(far, far, c_send.at[c], c_recv.at[c, 7], at(0, 1))

    def stage_3(c):
        wait(gat.at[c, rid(-1, 1)], c_recv.at[c, 3])
        wait(gat.at[c, rid(1, 1)], c_recv.at[c, 4])
        wait(gat.at[c, rid(2, 1)], c_recv.at[c, 7])
        squares = None
        for s in range(reps):
            v = gat[c, s, :, 0:WIDTH].astype(F32)
            part = jnp.sum(v * v, axis=1, keepdims=True)
            squares = part if s == 0 else squares + part
        scale = 1.0 / jnp.sqrt(squares / features + EPSILON)
        hidden_grad = None
        for s in range(reps):
            cols = slice(WIDTH * s, WIDTH * s + WIDTH)
            v = gat[c, s, :, 0:WIDTH].astype(F32)
            nrm[c, :, cols] = (v * gain_ref[:, cols] * scale).astype(BF16)
            part = dot(gat[c, s, :, WIDTH : 2 * WIDTH], wd[:, cols], (1, 1))
            hidden_grad = part if s == 0 else hidden_grad + part
        gate_pre = dot(nrm[c], wg[...], (1, 1))
        up_pre = dot(nrm[c], wu[...], (1, 1))
        sig = jax.nn.sigmoid(gate_pre)
        activated = gate_pre * sig
        hidden = (activated * up_pre).astype(BF16)
        gate_grad = (hidden_grad * up_pre * sig * (1.0 + gate_pre * (1.0 - sig))).astype(BF16)
        up_grad = (hidden_grad * activated).astype(BF16)
        hid[c], ggr[c], ugr[c] = hidden, gate_grad, up_grad
        for s in range(reps):
            cols = slice(WIDTH * s, WIDTH * s + WIDTH)
            par[c, s, :, 0:WIDTH] = dot(hidden, wd[:, cols], (1, 0)).astype(BF16)
            par[c, s, :, WIDTH : 2 * WIDTH] = (
                dot(gate_grad, wg[:, cols], (1, 0)) + dot(up_grad, wu[:, cols], (1, 0))
            ).astype(BF16)
        send(par.at[c, rid(2, 1)], got.at[c, 0], e_send.at[c], e_recv.at[c, 0], at(0, 1))
        send(par.at[c, rid(1, 1)], got.at[c, 1], e_send.at[c], e_recv.at[c, 1], at(1, 0))
        send(par.at[c, rid(-1, 1)], got.at[c, 2], e_send.at[c], e_recv.at[c, 2], at(-1, 0))

    def stage_4(c):
        far, other = rid(2, 0), rid(0, 1)
        wait(got.at[c, 0], e_recv.at[c, 0])
        par[c, far] = (par[c, far].astype(F32) + got[c, 0].astype(F32)).astype(BF16)
        send(par.at[c, far, low, :], got.at[c, 3, low, :], e_send.at[c], e_recv.at[c, 3], at(1, 0))
        send(par.at[c, far, high, :], got.at[c, 3, high, :], e_send.at[c], e_recv.at[c, 7], at(-1, 0))
        wait(got.at[c, 1], e_recv.at[c, 1])
        wait(got.at[c, 2], e_recv.at[c, 2])
        par[c, other] = (
            par[c, other].astype(F32) + got[c, 1].astype(F32) + got[c, 2].astype(F32)
        ).astype(BF16)
        send(par.at[c, other], got.at[c, 6], e_send.at[c], e_recv.at[c, 6], at(0, 1))

    def stage_5(c):
        right, left = rid(1, 0), rid(-1, 0)
        wait(got.at[c, 3, low, :], e_recv.at[c, 3])
        par[c, right, low, :] = (par[c, right, low, :].astype(F32) + got[c, 3, low, :].astype(F32)).astype(BF16)
        send(par.at[c, right], got.at[c, 4], e_send.at[c], e_recv.at[c, 4], at(1, 0))
        wait(got.at[c, 3, high, :], e_recv.at[c, 7])
        par[c, left, high, :] = (par[c, left, high, :].astype(F32) + got[c, 3, high, :].astype(F32)).astype(BF16)
        send(par.at[c, left], got.at[c, 5], e_send.at[c], e_recv.at[c, 5], at(-1, 0))

    def stage_6(c):
        total = par[c, rep].astype(F32)
        for k in (6, 4, 5):
            wait(got.at[c, k], e_recv.at[c, k])
            total = total + got[c, k].astype(F32)
        tiles = to_tiles(total.astype(BF16))
        fout[c] = tiles

        @pl.when(c != FIFTH)
        def _():
            send_tiles(fout, fback, f_send, f_recv, c, -1)

        @pl.when(c == 0)
        def _():
            fback[0, own_tile, :] = tiles[own_tile, :]

        @pl.when(c == FIFTH)
        def _():
            fback[FIFTH, own_fifth, :] = tiles[own_fifth, :]
            send_fifth(fout, fback, f_send, f_recv, -1)

    def stage_7(c):
        wait_tiles(fback, f_recv, c)
        tiles = fback[c]

        @pl.when(c != FIFTH)
        def _():
            for part in range(4):
                cols = slice(128 * part, 128 * part + 128)
                rows_in[c, :, cols] = dot(spread(part, False), tiles, (1, 0)).astype(BF16)

        @pl.when(c == FIFTH)
        def _():
            for part in range(4):
                cols = slice(128 * part, 128 * part + 128)
                rows = dot(spread(part, True), tiles, (1, 0)).astype(BF16)
                rows_in[FIFTH, 0:16, cols] = rows[0:16, :]
                for d in range(1, NJ):
                    loc[d, :, cols] = rows[16 * d : 16 * d + 16, :]
            for d in range(1, NJ):
                rows = slice(16 * d, 16 * d + 16)
                send(loc.at[d], rows_in.at[FIFTH, rows, :], l_send, l_recv, at_place(0, d))

    def turned(ref):
        return jnp.transpose(ref[...].reshape(CHUNKS * ROWS, ref.shape[2]).astype(F32)).astype(BF16)

    def update(s):
        cols = pl.ds(pl.multiple_of(s * WIDTH, WIDTH), WIDTH)
        rows_n = nrm[:, :, cols].reshape(CHUNKS * ROWS, WIDTH)
        rows_g = gat[:, s, :, WIDTH : 2 * WIDTH].reshape(CHUNKS * ROWS, WIDTH)
        gu[:, cols] = dot(ggt[...], rows_n, (1, 0)).astype(BF16)
        uu[:, cols] = dot(ugt[...], rows_n, (1, 0)).astype(BF16)
        du[:, cols] = dot(ht[...], rows_g, (1, 0)).astype(BF16)

    stages = (
        (9, stage_7), (6, stage_6), (5, stage_5), (4, stage_4), (3, stage_3), (2, stage_2), (1, stage_1), (0, stage_0)
    )
    first_free = CHUNKS + 3
    ticks = CHUNKS + stages[0][0]
    per_tick = 2

    def tick(t, carry):
        for lag, stage in reversed(stages):
            pl.when((t >= lag) & (t - lag < CHUNKS))(functools.partial(stage, t - lag))
        pl.when(t == 0)(hand_on)
        pl.when(t == 1)(send_fifth_rows)

        @pl.when(t == first_free)
        def _():
            ht[...], ggt[...], ugt[...] = turned(hid), turned(ggr), turned(ugr)

        @pl.when((t >= first_free) & (t < first_free + reps // per_tick))
        def _():
            for s in range(per_tick):
                update((t - first_free) * per_tick + s)

        return carry

    lax.fori_loop(0, ticks, tick, 0)

    updates = [
        pltpu.make_async_copy(gu, gu_out, o_sem.at[0]),
        pltpu.make_async_copy(uu, uu_out, o_sem.at[1]),
        pltpu.make_async_copy(du, du_out, o_sem.at[2]),
    ]
    for copy in updates:
        copy.start()

    r = iota((ROWS, 1), 0)
    codes = [
        code_of(choose(r & 15, ALL), r >> 4, jnp.full_like(r, 4)) if c == FIFTH
        else code_of(choose(r >> 4, OFFSETS[c]), (r >> 2) & 3, r & 3)
        for c in range(CHUNKS)
    ]
    ones = [
        jnp.concatenate([(code == meta[0, k : k + 1, :]).astype(F32).astype(BF16) for code in codes], axis=0)
        for k in range(2)
    ]
    grad = tok[0, :, WIDTH:].astype(F32)
    diagonal = iota((128, 128), 0) == iota((128, 128), 1)
    w = [jnp.sum(jnp.where(diagonal, meta[0, 2 + k : 3 + k, :], 0.0), axis=1, keepdims=True) for k in range(2)]
    wait(hx.at[pl.ds(0, reps - 1)], hx_recv)
    squares = None
    for s in range(reps):
        v = hx[s].astype(F32)
        part = jnp.sum(v * v, axis=1, keepdims=True)
        squares = part if s == 0 else squares + part
    root = jnp.sqrt(squares / features + EPSILON)

    wait(rows_in.at[FIFTH, 16:64, :], l_recv)
    rows = rows_in[...].reshape(CHUNKS * ROWS, 2 * WIDTH)
    picked = [dot(one, rows, (0, 0)) for one in ones]
    out_rows = [p[:, 0:WIDTH] for p in picked]
    share_out = (w[0] * out_rows[0] + w[1] * out_rows[1]).astype(BF16)
    share_in = (picked[0][:, WIDTH:] + picked[1][:, WIDTH:]).astype(BF16)
    dots = [jnp.sum(p * grad, axis=1, keepdims=True) for p in out_rows]
    heads = [d.astype(BF16).astype(F32) for d in dots]
    lane = iota((128, WIDTH), 1)
    products = jnp.where(
        lane == 0, heads[0],
        jnp.where(lane == 1, heads[1], jnp.where(lane == 2, dots[0] - heads[0], jnp.where(lane == 3, dots[1] - heads[1], 0.0))),
    ).astype(BF16)
    for s in range(reps):
        rows = slice(share * s, share * s + share)
        fin[s, 0:share, :] = share_out[rows, :]
        fin[s, share : 2 * share, :] = share_in[rows, :]
        fin[s, 2 * share :, :] = products[rows, :]
    for ro in range(1, reps):
        send(fin.at[rid(ro // 2, ro % 2)], fin_in.at[rep], y_send, y_recv, at(ro // 2, ro % 2))
    fin_in[rep] = fin[rep]

    wait(fin_in.at[pl.ds(0, reps - 1)], y_recv)
    inner = route = None
    for s in range(reps):
        cols = slice(WIDTH * s, WIDTH * s + WIDTH)
        v = hx[s].astype(F32)
        lo_ref[:, cols] = (v + fin_in[s, 0:share, :].astype(F32)).astype(BF16)
        scaled = gain_ref[:, cols] * fin_in[s, share : 2 * share, :].astype(F32)
        part = jnp.sum(scaled * v, axis=1, keepdims=True)
        inner = part if s == 0 else inner + part
        part = fin_in[s, 2 * share :, 0:128].astype(F32)
        route = part if s == 0 else route + part
    coefficient = inner / (features * root * root * root)
    for s in range(reps):
        cols = slice(WIDTH * s, WIDTH * s + WIDTH)
        scaled = gain_ref[:, cols] * fin_in[s, share : 2 * share, :].astype(F32)
        ig_ref[:, cols] = (scaled / root - hx[s].astype(F32) * coefficient).astype(BF16)
    diagonal = iota((share, share), 0) == iota((share, share), 1)
    for k in range(2):
        column = route[:, k : k + 1] + route[:, 2 + k : 3 + k]
        rg_ref[k : k + 1, :] = jnp.sum(jnp.where(diagonal, column, 0.0), axis=0, keepdims=True)

    wait(meta.at[1:NJ], meta_send)
    wait(tok.at[1:NJ], tok_send)
    wait(hx.at[pl.ds(0, reps - 1)], hx_send)
    for c in range(CHUNKS):
        sent = slice(0, 240 if c in (0, FIFTH) else 256)
        wait(zout.at[c, sent, :], z_send.at[c])
        wait(fout.at[c, sent, :], f_send.at[c])
    for c in range(CHUNKS):
        wait(gat.at[c, pl.ds(0, 7)], c_send.at[c])
        wait(got.at[c], e_send.at[c])
    wait(loc.at[1:NJ], l_send)
    wait(fin.at[pl.ds(0, reps - 1)], y_send)
    for copy in updates:
        copy.wait()


def hand_out(*refs):
    n = (len(refs) - 2) // 3
    sources, results, held, in_sem, out_sem = refs[:n], refs[n : 2 * n], refs[2 * n : 3 * n], refs[-2], refs[-1]
    pieces = [(i, slice(96 * k, 96 * k + 96)) for i in range(3, n) for k in range(2)]
    pieces += [(i, slice(None)) for i in range(3)]
    arriving, leaving = [], []
    for k, (i, rows) in enumerate(pieces):
        arriving.append(pltpu.make_async_copy(sources[i].at[rows, :], held[i].at[rows, :], in_sem.at[k]))
        arriving[-1].start()
    for k, (i, rows) in enumerate(pieces):
        arriving[k].wait()
        leaving.append(pltpu.make_async_copy(held[i].at[rows, :], results[i].at[rows, :], out_sem.at[k]))
        leaving[-1].start()
    for copy in leaving:
        copy.wait()


def body(hidden_in, norm_gain, route_ids, route_weights, w_gate, w_up, w_down, out_grad):
    reps = lax.axis_size("rep")
    units, features = w_gate.shape[1:]
    tokens = hidden_in.shape[0]
    share = tokens // reps
    vmem = pl.BlockSpec(memory_space=pltpu.VMEM)
    hbm = pl.BlockSpec(memory_space=pltpu.HBM)
    anywhere = pl.BlockSpec(memory_space=pl.ANY)
    matrix = pltpu.VMEM((units, features), BF16)
    dma = pltpu.SemaphoreType.DMA
    rows = CHUNKS * ROWS
    scratch = [matrix] * 6 + [
        pltpu.VMEM((NJ, tokens, 2 * WIDTH), BF16),
        pltpu.VMEM((NJ, 8, tokens), F32),
        pltpu.VMEM((reps, share, WIDTH), BF16),
        pltpu.VMEM((CHUNKS, 4 * ROWS, 128), BF16),
        pltpu.VMEM((CHUNKS, 4 * ROWS, 128), BF16),
        pltpu.VMEM((CHUNKS, reps, ROWS, 2 * WIDTH), BF16),
        pltpu.VMEM((CHUNKS, ROWS, features), BF16),
        pltpu.VMEM((CHUNKS, reps, ROWS, 2 * WIDTH), BF16),
        pltpu.VMEM((CHUNKS, 7, ROWS, 2 * WIDTH), BF16),
        pltpu.VMEM((CHUNKS, 4 * ROWS, 128), BF16),
        pltpu.VMEM((CHUNKS, 4 * ROWS, 128), BF16),
        pltpu.VMEM((NJ, 16, 2 * WIDTH), BF16),
        pltpu.VMEM((CHUNKS, ROWS, 2 * WIDTH), BF16),
        pltpu.VMEM((reps, 3 * share, WIDTH), BF16),
        pltpu.VMEM((reps, 3 * share, WIDTH), BF16),
    ]
    scratch += [pltpu.VMEM((CHUNKS, ROWS, units), BF16)] * 3
    scratch += [pltpu.VMEM((units, rows), BF16)] * 3
    scratch += [
        dma((3,)), dma((3,)), dma((2,)),
        dma, dma, dma, dma((3,)),
        dma, dma,
        dma((CHUNKS,)), dma((CHUNKS,)),
        dma((CHUNKS,)), dma((CHUNKS, 8)),
        dma((CHUNKS,)), dma((CHUNKS, 8)),
        dma((CHUNKS,)), dma((CHUNKS,)),
        dma, dma,
        dma, dma,
    ]
    update = jax.ShapeDtypeStruct((units, features), BF16)
    kinds = (
        jax.ShapeDtypeStruct((share, features), BF16),
        jax.ShapeDtypeStruct((share, features), BF16),
        jax.ShapeDtypeStruct((2, share), F32),
        update, update, update,
    )
    outs = pl.pallas_call(
        kernel,
        out_shape=kinds,
        in_specs=[hbm] * 2 + [vmem] * 3 + [hbm] * 3,
        out_specs=(vmem, vmem, vmem, anywhere, anywhere, anywhere),
        scratch_shapes=scratch,
        compiler_params=pltpu.CompilerParams(
            collective_id=0, has_side_effects=True, vmem_limit_bytes=62 * 1024 * 1024
        ),
        name="expert_layer",
    )(
        hidden_in, out_grad, route_ids.T, route_weights.T, norm_gain[None, :], w_gate[0], w_up[0], w_down[0]
    )
    outs = pl.pallas_call(
        hand_out,
        out_shape=kinds,
        in_specs=[anywhere] * 6,
        out_specs=(anywhere,) * 6,
        scratch_shapes=[pltpu.VMEM(kind.shape, kind.dtype) for kind in kinds] + [dma((9,)), dma((9,))],
        name="results",
    )(*outs)
    layer_out, input_grad, route_grad, gate_update, up_update, down_update = outs
    return layer_out, input_grad, route_grad.T, gate_update[None], up_update[None], down_update[None]


def solution(mesh):
    placed = (
        P("exp", "rep"),
        P(),
        P("exp", None),
        P("exp", None),
        P("exp", "rep", None),
        P("exp", "rep", None),
        P("exp", "rep", None),
        P("exp", "rep"),
    )
    return jax.shard_map(
        body,
        mesh=mesh,
        in_specs=placed,
        out_specs=(
            P(("exp", "rep"), None),
            P(("exp", "rep"), None),
            P(("exp", "rep"), None),
            P("exp", "rep", None),
            P("exp", "rep", None),
            P("exp", "rep", None),
        ),
        check_vma=False,
    )
```

```python
import functools

import jax
import jax.numpy as jnp
from jax import lax
from jax.experimental import pallas as pl
from jax.experimental.pallas import tpu as pltpu
from jax.sharding import PartitionSpec as P

LOGICAL = pl.DeviceIdType.LOGICAL
EPSILON = 1e-06
NZ = 16
NJ = 4
WIDTH = 256
CHUNKS = 5
ROWS = 64
F32 = jnp.float32
BF16 = jnp.bfloat16


OFFSETS = ((0, 3, 13, 4), (7, 9, 8, 10), None, (5, 11, 6, 12), (1, 2, 14, 15))
FIFTH = OFFSETS.index(None)
MAIN = tuple(c for c in range(CHUNKS) if c != FIFTH)
ALL = sum((OFFSETS[c] for c in MAIN), ())
HOME = next(c for c in MAIN if 0 in OFFSETS[c])
OWN_TILE = slice(64 * OFFSETS[HOME].index(0), 64 * OFFSETS[HOME].index(0) + 16)
OWN_FIFTH = slice(16 * ALL.index(0), 16 * ALL.index(0) + 16)


def choose(index, values):
    out = jnp.full_like(index, values[0])
    for i in range(1, len(values)):
        out = jnp.where(index == i, values[i], out)
    return out


def z_offset(c, m):
    if isinstance(c, int):
        return OFFSETS[c][m]
    return choose(c, [OFFSETS[i][m] if i != FIFTH else 0 for i in range(CHUNKS)])


def iota(shape, dim):
    return lax.broadcasted_iota(jnp.int32, shape, dim)


def dot(a, b, dims):
    return lax.dot_general(a, b, ((dims[:1], dims[1:]), ((), ())), preferred_element_type=F32)


def kernel(
    h_hbm, g_hbm, ids_ref, wrow_ref, gain_ref, wg_hbm, wu_hbm, wd_hbm,
    lo_ref, ig_ref, rg_ref, gu_out, uu_out, du_out,
    wg, wu, wd, gu, uu, du,
    tok, meta, hx, zout, zin, gat, nrm, par, got, fout, fback, loc, fifth_in, picked, fin, fin_in,
    hid, ggr, ugr, ht, ggt, ugt,
    w_sem, o_sem, own_sem, meta_send, meta_recv, tok_send, tok_recv, hx_send, hx_recv,
    z_send, z_recv, c_send, c_recv, e_send, e_recv, f_send, f_recv, l_send, l_recv, y_send, y_recv,
):
    reps = lax.axis_size("rep")
    features = reps * WIDTH
    share = h_hbm.shape[0] // reps
    rep = lax.axis_index("rep")
    exp = lax.axis_index("exp")
    z, j = exp // NJ, exp % NJ
    columns = reps // 2
    x, y = rep // 2, rep % 2

    here = rep * (NZ * NJ)
    planes = [lax.rem(j // 2 + d // 2, 2) * 2 + lax.rem(j % 2 + d % 2, 2) for d in range(NJ)]
    ids_z = [here + lax.rem(z + off, NZ) * NJ for off in range(NZ)]
    slots = {
        (dx, dy): lax.rem(x + columns + dx, columns) * 2 + lax.rem(y + dy, 2) for dx in (-1, 0, 1, 2) for dy in (0, 1)
    }

    def in_plane(d):
        return planes[d]

    def at_place(off, d):
        if isinstance(off, int):
            return ids_z[off % NZ] + planes[d]
        return here + lax.rem(z + off, NZ) * NJ + planes[d]

    def rid(dx, dy):
        return slots[(dx + 1) % columns - 1, dy]

    def at(dx, dy):
        return rid(dx, dy) * (NZ * NJ) + exp

    def send(src, dst, ssem, rsem, device):
        pltpu.make_async_remote_copy(
            src_ref=src, dst_ref=dst, send_sem=ssem, recv_sem=rsem, device_id=device, device_id_type=LOGICAL
        ).start()

    def wait(ref, sem):
        pltpu.make_async_copy(ref, ref, sem).wait()

    own = [
        pltpu.make_async_copy(h_hbm, tok.at[0, :, 0:WIDTH], own_sem.at[0]),
        pltpu.make_async_copy(g_hbm, tok.at[0, :, WIDTH : 2 * WIDTH], own_sem.at[1]),
    ]
    weights = [
        pltpu.make_async_copy(wg_hbm, wg, w_sem.at[0]),
        pltpu.make_async_copy(wu_hbm, wu, w_sem.at[1]),
        pltpu.make_async_copy(wd_hbm, wd, w_sem.at[2]),
    ]
    for copy in own + weights:
        copy.start()

    barrier = pltpu.get_barrier_semaphore()

    def greet(i, carry):
        off = 1 + lax.rem(i + 20, NZ * NJ - 1)
        pl.semaphore_signal(barrier, inc=1, device_id=here + lax.rem(exp + off, NZ * NJ), device_id_type=LOGICAL)
        return carry

    lax.fori_loop(0, NZ * NJ - 1, greet, 0)
    for ro in range(1, reps):
        pl.semaphore_signal(barrier, inc=1, device_id=at(ro // 2, ro % 2), device_id_type=LOGICAL)

    ids = ids_ref[...]
    expert_rows = iota((NZ * NJ, 128), 0)
    hits = [(expert_rows == ids[k : k + 1, :]).astype(F32) for k in range(2)]
    before = (iota((128, 128), 0) < iota((128, 128), 1)).astype(F32).astype(BF16)
    earlier = dot((hits[0] + hits[1]).astype(BF16), before, (1, 0))
    for k in range(2):
        number = jnp.sum(hits[k] * earlier, axis=0, keepdims=True)
        meta[0, k : k + 1, :] = ids[k : k + 1, :].astype(F32) * 8.0 + number
    meta[0, 2:4, :] = wrow_ref[...]
    meta[0, 4:8, :] = jnp.zeros((4, 128), F32)

    for copy in own:
        copy.wait()

    def code_of(off, place, number):
        plane = (z + off) & (NZ - 1)
        return ((plane * NJ + choose(place, [in_plane(d) for d in range(NJ)])) * 8 + number).astype(F32)

    r = iota((4 * ROWS, 1), 0)
    part_of = (r >> 2) & 3
    blocks = jnp.concatenate([tok[0, :, 128 * f : 128 * f + 128] for f in range(4)], axis=0)

    def pick(code, d):
        one = [code == meta[d, k : k + 1, :] for k in range(2)]
        w = jnp.where(one[0], meta[d, 2:3, :], 0.0) + jnp.where(one[1], meta[d, 3:4, :], 0.0)
        return (one[0] | one[1]).astype(F32), jnp.sum(w, axis=1, keepdims=True)

    def build(c):
        hit, weight = pick(code_of(choose(r >> 6, OFFSETS[c]), (r >> 4) & 3, r & 3), 0)
        masks = jnp.concatenate([jnp.where(part_of == f, hit, 0.0) for f in range(4)], axis=1).astype(BF16)
        tiles = dot(masks, blocks, (1, 0))
        zout[c] = jnp.where(part_of >= 2, weight * tiles, tiles).astype(BF16)

    build(MAIN[0])
    pl.semaphore_wait(barrier, NZ * NJ - 1 + reps - 1)

    def send_tiles(src, dst, ssem, rsem, c, sign):
        for m in range(4):
            off = z_offset(c, m)
            off = off if sign > 0 else NZ - off
            for d in range(NJ):
                rows = slice(64 * m + 16 * d, 64 * m + 16 * d + 16)

                def far(rows=rows, d=d, off=off):
                    send(src.at[c, rows, :], dst.at[c, rows, :], ssem.at[c], rsem.at[c], at_place(off, d))

                if OFFSETS[HOME][m] == 0 and d == 0:
                    if not isinstance(c, int):
                        pl.when(c != HOME)(far)
                    elif c != HOME:
                        far()
                else:
                    far()

    def send_fifth(src, dst, ssem, rsem, sign):
        for place, off in enumerate(ALL):
            if off != 0:
                rows = slice(16 * place, 16 * place + 16)
                to = at_place(off if sign > 0 else NZ - off, 0)
                send(src.at[FIFTH, rows, :], dst.at[FIFTH, rows, :], ssem.at[FIFTH], rsem.at[FIFTH], to)

    send_tiles(zout, zin, z_send, z_recv, MAIN[0], 1)

    for d in (2, 3, 1):
        send(meta.at[0], meta.at[d], meta_send, meta_recv, at_place(0, d))
    send(tok.at[0], tok.at[2], tok_send, tok_recv.at[1], at_place(0, 2))
    send(tok.at[0], tok.at[1], tok_send, tok_recv.at[0], at_place(0, 1))
    for c in MAIN[1:]:
        build(c)
        send_tiles(zout, zin, z_send, z_recv, c, 1)
    zin[HOME, OWN_TILE, :] = zout[HOME, OWN_TILE, :]

    def hand_on():
        wait(tok.at[2], tok_recv.at[1])
        send(tok.at[2], tok.at[3], tok_send, tok_recv.at[2], at_place(0, 1))

    def spread(part, to_blocks):
        r, t = iota((ROWS, 4 * ROWS), 0), iota((ROWS, 4 * ROWS), 1)
        tile, d = (r & 15, r >> 4) if to_blocks else (r >> 2, r & 3)
        return (t == 16 * tile + 4 * part + d).astype(F32).astype(BF16)

    def to_tiles(rows):
        tiles = None
        for part in range(4):
            one = dot(spread(part, False), rows[:, 128 * part : 128 * part + 128], (0, 0))
            tiles = one if part == 0 else tiles + one
        return tiles.astype(BF16)

    def send_fifth_rows():
        wait(meta.at[1:NJ], meta_recv)
        wait(tok.at[1], tok_recv.at[0])
        wait(tok.at[3], tok_recv.at[2])
        r = iota((ROWS, 1), 0)
        code = code_of(choose(r >> 2, ALL), jnp.zeros_like(r), jnp.full_like(r, 4))
        rows = weight = None
        for d in range(NJ):
            hit, w = pick(jnp.where((r & 3) == d, code, -1.0), d)
            one = dot(hit.astype(BF16), tok[d], (1, 0))
            rows = one if d == 0 else rows + one
            weight = w if d == 0 else weight + w
        lanes = iota((1, 2 * WIDTH), 1)
        tiles = to_tiles(jnp.where(lanes < WIDTH, rows, weight * rows).astype(BF16))
        zout[FIFTH] = tiles
        zin[FIFTH, OWN_FIFTH, :] = tiles[OWN_FIFTH, :]
        send_fifth(zout, zin, z_send, z_recv, 1)

    for ro in range(1, reps):
        to = rid(ro // 2, ro % 2)
        rows = pl.ds(pl.multiple_of(to * share, 16), share)
        send(tok.at[0, rows, 0:WIDTH], hx.at[rep], hx_send, hx_recv, at(ro // 2, ro % 2))
    hx[rep] = tok[0, pl.ds(pl.multiple_of(rep * share, 16), share), 0:WIDTH]

    for copy in weights:
        copy.wait()

    low, high = slice(0, ROWS // 2), slice(ROWS // 2, ROWS)

    def gather(c):
        mine = gat.at[c, rep]
        send(mine, mine, c_send.at[c], c_recv.at[c, 0], at(0, 1))
        send(mine, mine, c_send.at[c], c_recv.at[c, 1], at(1, 0))
        send(mine, mine, c_send.at[c], c_recv.at[c, 2], at(-1, 0))

    def wait_tiles(ref, sem, c):
        fewer = (c == HOME) | (c == FIFTH)

        @pl.when(fewer)
        def _():
            wait(ref.at[c, 0:240, :], sem.at[c])

        @pl.when(jnp.logical_not(fewer))
        def _():
            wait(ref.at[c], sem.at[c])

    def stage_0(c):
        wait_tiles(zin, z_recv, c)
        tiles = zin[c]
        for part in range(4):
            cols = slice(128 * part, 128 * part + 128)
            gat[c, rep, :, cols] = dot(spread(part, False), tiles, (1, 0)).astype(BF16)
        gather(c)

    def stage_1(c):
        other, left, right = gat.at[c, rid(0, 1)], gat.at[c, rid(-1, 0)], gat.at[c, rid(1, 0)]
        wait(other, c_recv.at[c, 0])
        send(other, other, c_send.at[c], c_recv.at[c, 3], at(1, 0))
        send(other, other, c_send.at[c], c_recv.at[c, 4], at(-1, 0))
        wait(left, c_recv.at[c, 1])
        send(left.at[low, :], left.at[low, :], c_send.at[c], c_recv.at[c, 5], at(1, 0))
        wait(right, c_recv.at[c, 2])
        send(right.at[high, :], right.at[high, :], c_send.at[c], c_recv.at[c, 6], at(-1, 0))

    def stage_2(c):
        far = gat.at[c, rid(2, 0)]
        wait(far.at[low, :], c_recv.at[c, 5])
        wait(far.at[high, :], c_recv.at[c, 6])
        send(far, far, c_send.at[c], c_recv.at[c, 7], at(0, 1))

    def stage_3(c):
        wait(gat.at[c, rid(-1, 1)], c_recv.at[c, 3])
        wait(gat.at[c, rid(1, 1)], c_recv.at[c, 4])
        wait(gat.at[c, rid(2, 1)], c_recv.at[c, 7])
        squares = None
        for s in range(reps):
            v = gat[c, s, :, 0:WIDTH].astype(F32)
            part = jnp.sum(v * v, axis=1, keepdims=True)
            squares = part if s == 0 else squares + part
        scale = 1.0 / jnp.sqrt(squares / features + EPSILON)
        hidden_grad = None
        for s in range(reps):
            cols = slice(WIDTH * s, WIDTH * s + WIDTH)
            v = gat[c, s, :, 0:WIDTH].astype(F32)
            nrm[c, :, cols] = (v * gain_ref[:, cols] * scale).astype(BF16)
            part = dot(gat[c, s, :, WIDTH : 2 * WIDTH], wd[:, cols], (1, 1))
            hidden_grad = part if s == 0 else hidden_grad + part
        gate_pre = dot(nrm[c], wg[...], (1, 1))
        up_pre = dot(nrm[c], wu[...], (1, 1))
        sig = jax.nn.sigmoid(gate_pre)
        activated = gate_pre * sig
        hidden = (activated * up_pre).astype(BF16)
        gate_grad = (hidden_grad * up_pre * sig * (1.0 + gate_pre * (1.0 - sig))).astype(BF16)
        up_grad = (hidden_grad * activated).astype(BF16)
        hid[c], ggr[c], ugr[c] = hidden, gate_grad, up_grad
        for s in range(reps):
            cols = slice(WIDTH * s, WIDTH * s + WIDTH)
            par[c, s, :, 0:WIDTH] = dot(hidden, wd[:, cols], (1, 0)).astype(BF16)
            par[c, s, :, WIDTH : 2 * WIDTH] = (
                dot(gate_grad, wg[:, cols], (1, 0)) + dot(up_grad, wu[:, cols], (1, 0))
            ).astype(BF16)
        send(par.at[c, rid(2, 1)], got.at[c, 0], e_send.at[c], e_recv.at[c, 0], at(0, 1))
        send(par.at[c, rid(1, 1)], got.at[c, 1], e_send.at[c], e_recv.at[c, 1], at(1, 0))
        send(par.at[c, rid(-1, 1)], got.at[c, 2], e_send.at[c], e_recv.at[c, 2], at(-1, 0))

    def stage_4(c):
        far, other = rid(2, 0), rid(0, 1)
        wait(got.at[c, 0], e_recv.at[c, 0])
        par[c, far] = (par[c, far].astype(F32) + got[c, 0].astype(F32)).astype(BF16)
        send(par.at[c, far, low, :], got.at[c, 3, low, :], e_send.at[c], e_recv.at[c, 3], at(1, 0))
        send(par.at[c, far, high, :], got.at[c, 3, high, :], e_send.at[c], e_recv.at[c, 7], at(-1, 0))
        wait(got.at[c, 1], e_recv.at[c, 1])
        wait(got.at[c, 2], e_recv.at[c, 2])
        par[c, other] = (
            par[c, other].astype(F32) + got[c, 1].astype(F32) + got[c, 2].astype(F32)
        ).astype(BF16)
        send(par.at[c, other], got.at[c, 6], e_send.at[c], e_recv.at[c, 6], at(0, 1))

    def stage_5(c):
        right, left = rid(1, 0), rid(-1, 0)
        wait(got.at[c, 3, low, :], e_recv.at[c, 3])
        par[c, right, low, :] = (par[c, right, low, :].astype(F32) + got[c, 3, low, :].astype(F32)).astype(BF16)
        send(par.at[c, right], got.at[c, 4], e_send.at[c], e_recv.at[c, 4], at(1, 0))
        wait(got.at[c, 3, high, :], e_recv.at[c, 7])
        par[c, left, high, :] = (par[c, left, high, :].astype(F32) + got[c, 3, high, :].astype(F32)).astype(BF16)
        send(par.at[c, left], got.at[c, 5], e_send.at[c], e_recv.at[c, 5], at(-1, 0))

    def stage_6(c):
        total = par[c, rep].astype(F32)
        for k in (6, 4, 5):
            wait(got.at[c, k], e_recv.at[c, k])
            total = total + got[c, k].astype(F32)
        tiles = to_tiles(total.astype(BF16))
        fout[c] = tiles

        @pl.when(c != FIFTH)
        def _():
            send_tiles(fout, fback, f_send, f_recv, c, -1)

        @pl.when(c == HOME)
        def _():
            fback[HOME, OWN_TILE, :] = tiles[OWN_TILE, :]

        @pl.when(c == FIFTH)
        def _():
            fback[FIFTH, OWN_FIFTH, :] = tiles[OWN_FIFTH, :]
            send_fifth(fout, fback, f_send, f_recv, -1)

    def add_rows(code, rows):
        for k in range(2):
            one = (code == meta[0, k : k + 1, :]).astype(F32).astype(BF16)
            picked[k] = picked[k] + dot(one, rows, (0, 0))

    def stage_7(c):
        wait_tiles(fback, f_recv, c)
        tiles = fback[c]

        @pl.when(c != FIFTH)
        def _():
            rows = [dot(spread(part, False), tiles, (1, 0)).astype(BF16) for part in range(4)]
            r = iota((ROWS, 1), 0)
            code = code_of(choose(r >> 4, [z_offset(c, m) for m in range(4)]), (r >> 2) & 3, r & 3)
            add_rows(code, jnp.concatenate(rows, axis=1))

        @pl.when(c == FIFTH)
        def _():
            for part in range(4):
                cols = slice(128 * part, 128 * part + 128)
                rows = dot(spread(part, True), tiles, (1, 0)).astype(BF16)
                fifth_in[0:16, cols] = rows[0:16, :]
                for d in range(1, NJ):
                    loc[d, :, cols] = rows[16 * d : 16 * d + 16, :]
            for d in range(1, NJ):
                rows = slice(16 * d, 16 * d + 16)
                send(loc.at[d], fifth_in.at[rows, :], l_send, l_recv, at_place(0, d))

    def turned(ref):
        return jnp.transpose(ref[...].reshape(CHUNKS * ROWS, ref.shape[2]).astype(F32)).astype(BF16)

    def update(s):
        cols = pl.ds(pl.multiple_of(s * WIDTH, WIDTH), WIDTH)
        rows_n = nrm[:, :, cols].reshape(CHUNKS * ROWS, WIDTH)
        rows_g = gat[:, s, :, WIDTH : 2 * WIDTH].reshape(CHUNKS * ROWS, WIDTH)
        gu[:, cols] = dot(ggt[...], rows_n, (1, 0)).astype(BF16)
        uu[:, cols] = dot(ugt[...], rows_n, (1, 0)).astype(BF16)
        du[:, cols] = dot(ht[...], rows_g, (1, 0)).astype(BF16)

    stages = (
        (9, stage_7), (6, stage_6), (5, stage_5), (4, stage_4), (3, stage_3), (2, stage_2), (1, stage_1), (0, stage_0)
    )
    first_free = CHUNKS + 3
    ticks = CHUNKS + stages[0][0]
    per_tick = 2

    def tick(t, carry):
        for lag, stage in reversed(stages):
            pl.when((t >= lag) & (t - lag < CHUNKS))(functools.partial(stage, t - lag))

        @pl.when(t == first_free)
        def _():
            ht[...], ggt[...], ugt[...] = turned(hid), turned(ggr), turned(ugr)

        @pl.when((t >= first_free) & (t < first_free + reps // per_tick))
        def _():
            for s in range(per_tick):
                update((t - first_free) * per_tick + s)

        return carry

    picked[...] = jnp.zeros_like(picked)
    hand_on()
    send_fifth_rows()
    lax.fori_loop(0, ticks, tick, 0)

    updates = [
        pltpu.make_async_copy(gu, gu_out, o_sem.at[0]),
        pltpu.make_async_copy(uu, uu_out, o_sem.at[1]),
        pltpu.make_async_copy(du, du_out, o_sem.at[2]),
    ]
    for copy in updates:
        copy.start()

    grad = tok[0, :, WIDTH:].astype(F32)
    diagonal = iota((128, 128), 0) == iota((128, 128), 1)
    w = [jnp.sum(jnp.where(diagonal, meta[0, 2 + k : 3 + k, :], 0.0), axis=1, keepdims=True) for k in range(2)]
    wait(hx.at[pl.ds(0, reps - 1)], hx_recv)
    squares = None
    for s in range(reps):
        v = hx[s].astype(F32)
        part = jnp.sum(v * v, axis=1, keepdims=True)
        squares = part if s == 0 else squares + part
    root = jnp.sqrt(squares / features + EPSILON)

    r = iota((ROWS, 1), 0)
    code = code_of(choose(r & 15, ALL), r >> 4, jnp.full_like(r, 4))
    wait(fifth_in.at[16:64, :], l_recv)
    add_rows(code, fifth_in[...])
    out_rows = [picked[k, :, 0:WIDTH] for k in range(2)]
    share_out = (w[0] * out_rows[0] + w[1] * out_rows[1]).astype(BF16)
    share_in = (picked[0, :, WIDTH:] + picked[1, :, WIDTH:]).astype(BF16)
    dots = [jnp.sum(p * grad, axis=1, keepdims=True) for p in out_rows]
    heads = [d.astype(BF16).astype(F32) for d in dots]
    lane = iota((128, 128), 1)
    products = jnp.where(
        lane == 0, heads[0],
        jnp.where(lane == 1, heads[1], jnp.where(lane == 2, dots[0] - heads[0], jnp.where(lane == 3, dots[1] - heads[1], 0.0))),
    ).astype(BF16)
    halves = [share_out[:, 0:128], share_out[:, 128:], share_in[:, 0:128], share_in[:, 128:], products]
    for s in range(reps):
        for i, half in enumerate(halves):
            fin[s, share * i : share * i + share, :] = half[share * s : share * s + share, :]
    for ro in range(1, reps):
        send(fin.at[rid(ro // 2, ro % 2)], fin_in.at[rep], y_send, y_recv, at(ro // 2, ro % 2))
    fin_in[rep] = fin[rep]

    wait(fin_in.at[pl.ds(0, reps - 1)], y_recv)
    inner = route = None
    for s in range(2 * reps):
        cols = slice(128 * s, 128 * s + 128)
        v = hx[s // 2, :, 128 * (s % 2) : 128 * (s % 2) + 128].astype(F32)
        at_out, at_in = share * (s % 2), share * (2 + s % 2)
        lo_ref[:, cols] = (v + fin_in[s // 2, at_out : at_out + share, :].astype(F32)).astype(BF16)
        scaled = gain_ref[:, cols] * fin_in[s // 2, at_in : at_in + share, :].astype(F32)
        part = jnp.sum(scaled * v, axis=1, keepdims=True)
        inner = part if s == 0 else inner + part
    for s in range(reps):
        part = fin_in[s, 4 * share :, :].astype(F32)
        route = part if s == 0 else route + part
    coefficient = inner / (features * root * root * root)
    for s in range(2 * reps):
        cols = slice(128 * s, 128 * s + 128)
        v = hx[s // 2, :, 128 * (s % 2) : 128 * (s % 2) + 128].astype(F32)
        at_in = share * (2 + s % 2)
        scaled = gain_ref[:, cols] * fin_in[s // 2, at_in : at_in + share, :].astype(F32)
        ig_ref[:, cols] = (scaled / root - v * coefficient).astype(BF16)
    diagonal = iota((share, share), 0) == iota((share, share), 1)
    for k in range(2):
        column = route[:, k : k + 1] + route[:, 2 + k : 3 + k]
        rg_ref[k : k + 1, :] = jnp.sum(jnp.where(diagonal, column, 0.0), axis=0, keepdims=True)

    wait(meta.at[1:NJ], meta_send)
    wait(tok.at[1:NJ], tok_send)
    wait(hx.at[pl.ds(0, reps - 1)], hx_send)
    for c in range(CHUNKS):
        sent = slice(0, 240 if c in (HOME, FIFTH) else 256)
        wait(zout.at[c, sent, :], z_send.at[c])
        wait(fout.at[c, sent, :], f_send.at[c])
    for c in range(CHUNKS):
        wait(gat.at[c, pl.ds(0, 7)], c_send.at[c])
        wait(got.at[c], e_send.at[c])
    wait(loc.at[1:NJ], l_send)
    wait(fin.at[pl.ds(0, reps - 1)], y_send)
    for copy in updates:
        copy.wait()


def hand_out(*refs):
    n = (len(refs) - 2) // 3
    sources, results, held, in_sem, out_sem = refs[:n], refs[n : 2 * n], refs[2 * n : 3 * n], refs[-2], refs[-1]
    pieces = [(i, slice(96 * k, 96 * k + 96)) for i in range(3, n) for k in range(2)]
    pieces += [(i, slice(None)) for i in range(3)]
    arriving, leaving = [], []
    for k, (i, rows) in enumerate(pieces):
        arriving.append(pltpu.make_async_copy(sources[i].at[rows, :], held[i].at[rows, :], in_sem.at[k]))
        arriving[-1].start()
    for k, (i, rows) in enumerate(pieces):
        arriving[k].wait()
        leaving.append(pltpu.make_async_copy(held[i].at[rows, :], results[i].at[rows, :], out_sem.at[k]))
        leaving[-1].start()
    for copy in leaving:
        copy.wait()


def body(hidden_in, norm_gain, route_ids, route_weights, w_gate, w_up, w_down, out_grad):
    reps = lax.axis_size("rep")
    units, features = w_gate.shape[1:]
    tokens = hidden_in.shape[0]
    share = tokens // reps
    vmem = pl.BlockSpec(memory_space=pltpu.VMEM)
    hbm = pl.BlockSpec(memory_space=pltpu.HBM)
    anywhere = pl.BlockSpec(memory_space=pl.ANY)
    matrix = pltpu.VMEM((units, features), BF16)
    dma = pltpu.SemaphoreType.DMA
    rows = CHUNKS * ROWS
    scratch = [matrix] * 6 + [
        pltpu.VMEM((NJ, tokens, 2 * WIDTH), BF16),
        pltpu.VMEM((NJ, 8, tokens), F32),
        pltpu.VMEM((reps, share, WIDTH), BF16),
        pltpu.VMEM((CHUNKS, 4 * ROWS, 128), BF16),
        pltpu.VMEM((CHUNKS, 4 * ROWS, 128), BF16),
        pltpu.VMEM((CHUNKS, reps, ROWS, 2 * WIDTH), BF16),
        pltpu.VMEM((CHUNKS, ROWS, features), BF16),
        pltpu.VMEM((CHUNKS, reps, ROWS, 2 * WIDTH), BF16),
        pltpu.VMEM((CHUNKS, 7, ROWS, 2 * WIDTH), BF16),
        pltpu.VMEM((CHUNKS, 4 * ROWS, 128), BF16),
        pltpu.VMEM((CHUNKS, 4 * ROWS, 128), BF16),
        pltpu.VMEM((NJ, 16, 2 * WIDTH), BF16),
        pltpu.VMEM((ROWS, 2 * WIDTH), BF16),
        pltpu.VMEM((2, tokens, 2 * WIDTH), F32),
        pltpu.VMEM((reps, 5 * share, 128), BF16),
        pltpu.VMEM((reps, 5 * share, 128), BF16),
    ]
    scratch += [pltpu.VMEM((CHUNKS, ROWS, units), BF16)] * 3
    scratch += [pltpu.VMEM((units, rows), BF16)] * 3
    scratch += [
        dma((3,)), dma((3,)), dma((2,)),
        dma, dma, dma, dma((3,)),
        dma, dma,
        dma((CHUNKS,)), dma((CHUNKS,)),
        dma((CHUNKS,)), dma((CHUNKS, 8)),
        dma((CHUNKS,)), dma((CHUNKS, 8)),
        dma((CHUNKS,)), dma((CHUNKS,)),
        dma, dma,
        dma, dma,
    ]
    update = jax.ShapeDtypeStruct((units, features), BF16)
    kinds = (
        jax.ShapeDtypeStruct((share, features), BF16),
        jax.ShapeDtypeStruct((share, features), BF16),
        jax.ShapeDtypeStruct((2, share), F32),
        update, update, update,
    )
    outs = pl.pallas_call(
        kernel,
        out_shape=kinds,
        in_specs=[hbm] * 2 + [vmem] * 3 + [hbm] * 3,
        out_specs=(vmem, vmem, vmem, anywhere, anywhere, anywhere),
        scratch_shapes=scratch,
        compiler_params=pltpu.CompilerParams(
            collective_id=0, has_side_effects=True, vmem_limit_bytes=62 * 1024 * 1024
        ),
        name="expert_layer",
    )(
        hidden_in, out_grad, route_ids.T, route_weights.T, norm_gain[None, :], w_gate[0], w_up[0], w_down[0]
    )
    outs = pl.pallas_call(
        hand_out,
        out_shape=kinds,
        in_specs=[anywhere] * 6,
        out_specs=(anywhere,) * 6,
        scratch_shapes=[pltpu.VMEM(kind.shape, kind.dtype) for kind in kinds] + [dma((9,)), dma((9,))],
        name="results",
    )(*outs)
    layer_out, input_grad, route_grad, gate_update, up_update, down_update = outs
    return layer_out, input_grad, route_grad.T, gate_update[None], up_update[None], down_update[None]


def solution(mesh):
    placed = (
        P("exp", "rep"),
        P(),
        P("exp", None),
        P("exp", None),
        P("exp", "rep", None),
        P("exp", "rep", None),
        P("exp", "rep", None),
        P("exp", "rep"),
    )
    return jax.shard_map(
        body,
        mesh=mesh,
        in_specs=placed,
        out_specs=(
            P(("exp", "rep"), None),
            P(("exp", "rep"), None),
            P(("exp", "rep"), None),
            P("exp", "rep", None),
            P("exp", "rep", None),
            P("exp", "rep", None),
        ),
        check_vma=False,
    )
```

```python
import functools

import jax
import jax.numpy as jnp
from jax import lax
from jax.experimental import pallas as pl
from jax.experimental.pallas import tpu as pltpu
from jax.sharding import PartitionSpec as P

LOGICAL = pl.DeviceIdType.LOGICAL
EPSILON = 1e-06
NZ = 16
NJ = 4
WIDTH = 256
CHUNKS = 5
ROWS = 64
F32 = jnp.float32
BF16 = jnp.bfloat16


OFFSETS = ((0, 3, 13, 4), (7, 9, 8, 10), None, (5, 11, 6, 12), (1, 2, 14, 15))
FIFTH = OFFSETS.index(None)
MAIN = tuple(c for c in range(CHUNKS) if c != FIFTH)
ALL = sum((OFFSETS[c] for c in MAIN), ())
HOME = next(c for c in MAIN if 0 in OFFSETS[c])
OWN_TILE = slice(64 * OFFSETS[HOME].index(0), 64 * OFFSETS[HOME].index(0) + 16)
OWN_FIFTH = slice(16 * ALL.index(0), 16 * ALL.index(0) + 16)


def choose(index, values):
    out = jnp.full_like(index, values[0])
    for i in range(1, len(values)):
        out = jnp.where(index == i, values[i], out)
    return out


def z_offset(c, m):
    if isinstance(c, int):
        return OFFSETS[c][m]
    return choose(c, [OFFSETS[i][m] if i != FIFTH else 0 for i in range(CHUNKS)])


def iota(shape, dim):
    return lax.broadcasted_iota(jnp.int32, shape, dim)


def dot(a, b, dims):
    return lax.dot_general(a, b, ((dims[:1], dims[1:]), ((), ())), preferred_element_type=F32)


def kernel(
    h_hbm, g_hbm, ids_hbm, wrow_hbm, gain_hbm, wg_hbm, wu_hbm, wd_hbm,
    lo_ref, ig_ref, rg_ref, gu_out, uu_out, du_out,
    wg, wu, wd, gu, uu, du,
    ids_ref, wrow_ref, gain_ref, spreads, tok, meta, hx, zout, zin, gat, nrm, par, got, fout, fback, loc, fifth_in, picked, fin, fin_in,
    hid, ggr, ugr, ht, ggt, ugt,
    w_sem, o_sem, own_sem, meta_send, meta_recv, tok_send, tok_recv, hx_send, hx_recv,
    z_send, z_recv, c_send, c_recv, e_send, e_recv, f_send, f_recv, l_send, l_recv, y_send, y_recv,
):
    reps = lax.axis_size("rep")
    features = reps * WIDTH
    share = h_hbm.shape[0] // reps
    rep = lax.axis_index("rep")
    exp = lax.axis_index("exp")
    z, j = exp // NJ, exp % NJ
    columns = reps // 2
    x, y = rep // 2, rep % 2

    here = rep * (NZ * NJ)
    planes = [lax.rem(j // 2 + d // 2, 2) * 2 + lax.rem(j % 2 + d % 2, 2) for d in range(NJ)]
    ids_z = [here + lax.rem(z + off, NZ) * NJ for off in range(NZ)]
    slots = {
        (dx, dy): lax.rem(x + columns + dx, columns) * 2 + lax.rem(y + dy, 2) for dx in (-1, 0, 1, 2) for dy in (0, 1)
    }

    def in_plane(d):
        return planes[d]

    def at_place(off, d):
        if isinstance(off, int):
            return ids_z[off % NZ] + planes[d]
        return here + lax.rem(z + off, NZ) * NJ + planes[d]

    def rid(dx, dy):
        return slots[(dx + 1) % columns - 1, dy]

    def at(dx, dy):
        return rid(dx, dy) * (NZ * NJ) + exp

    def send(src, dst, ssem, rsem, device):
        pltpu.make_async_remote_copy(
            src_ref=src, dst_ref=dst, send_sem=ssem, recv_sem=rsem, device_id=device, device_id_type=LOGICAL
        ).start()

    def wait(ref, sem):
        pltpu.make_async_copy(ref, ref, sem).wait()

    routes = [
        pltpu.make_async_copy(ids_hbm, ids_ref, own_sem.at[2]),
        pltpu.make_async_copy(wrow_hbm, wrow_ref, own_sem.at[3]),
        pltpu.make_async_copy(gain_hbm, gain_ref, own_sem.at[4]),
    ]
    own = [
        pltpu.make_async_copy(h_hbm, tok.at[0, :, 0:WIDTH], own_sem.at[0]),
        pltpu.make_async_copy(g_hbm, tok.at[0, :, WIDTH : 2 * WIDTH], own_sem.at[1]),
    ]
    weights = [
        pltpu.make_async_copy(wg_hbm, wg, w_sem.at[0]),
        pltpu.make_async_copy(wu_hbm, wu, w_sem.at[1]),
        pltpu.make_async_copy(wd_hbm, wd, w_sem.at[2]),
    ]
    for copy in routes + own + weights:
        copy.start()

    barrier = pltpu.get_barrier_semaphore()

    for off in sorted(range(NZ), key=lambda off: -min(off, NZ - off)):
        for d in range(NJ):
            if off or d:
                pl.semaphore_signal(barrier, inc=1, device_id=at_place(off, d), device_id_type=LOGICAL)
    for ro in range(1, reps):
        pl.semaphore_signal(barrier, inc=1, device_id=at(ro // 2, ro % 2), device_id_type=LOGICAL)

    for copy in routes:
        copy.wait()
    ids = ids_ref[...]
    expert_rows = iota((NZ * NJ, 128), 0)
    hits = [(expert_rows == ids[k : k + 1, :]).astype(F32) for k in range(2)]
    before = (iota((128, 128), 0) < iota((128, 128), 1)).astype(F32).astype(BF16)
    earlier = dot((hits[0] + hits[1]).astype(BF16), before, (1, 0))
    for k in range(2):
        number = jnp.sum(hits[k] * earlier, axis=0, keepdims=True)
        meta[0, k : k + 1, :] = ids[k : k + 1, :].astype(F32) * 8.0 + number
    meta[0, 2:4, :] = wrow_ref[...]
    meta[0, 4:8, :] = jnp.zeros((4, 128), F32)

    for copy in own:
        copy.wait()

    def code_of(off, place, number):
        plane = (z + off) & (NZ - 1)
        return ((plane * NJ + choose(place, [in_plane(d) for d in range(NJ)])) * 8 + number).astype(F32)

    r = iota((4 * ROWS, 1), 0)
    part_of = (r >> 2) & 3
    blocks = jnp.concatenate([tok[0, :, 128 * f : 128 * f + 128] for f in range(4)], axis=0)

    def pick(code, d):
        one = [code == meta[d, k : k + 1, :] for k in range(2)]
        w = jnp.where(one[0], meta[d, 2:3, :], 0.0) + jnp.where(one[1], meta[d, 3:4, :], 0.0)
        return (one[0] | one[1]).astype(F32), jnp.sum(w, axis=1, keepdims=True)

    def build(c):
        hit, weight = pick(code_of(choose(r >> 6, OFFSETS[c]), (r >> 4) & 3, r & 3), 0)
        masks = jnp.concatenate([jnp.where(part_of == f, hit, 0.0) for f in range(4)], axis=1).astype(BF16)
        tiles = dot(masks, blocks, (1, 0))
        zout[c] = jnp.where(part_of >= 2, weight * tiles, tiles).astype(BF16)

    build(MAIN[0])
    row, col = iota((ROWS, 4 * ROWS), 0), iota((ROWS, 4 * ROWS), 1)
    for part in range(4):
        spreads[part] = (col == 16 * (row >> 2) + 4 * part + (row & 3)).astype(F32).astype(BF16)
    pl.semaphore_wait(barrier, NZ * NJ - 1 + reps - 1)

    def send_tiles(src, dst, ssem, rsem, c, sign):
        for m in range(4):
            off = z_offset(c, m)
            off = off if sign > 0 else NZ - off
            for d in range(NJ):
                rows = slice(64 * m + 16 * d, 64 * m + 16 * d + 16)

                def far(rows=rows, d=d, off=off):
                    send(src.at[c, rows, :], dst.at[c, rows, :], ssem.at[c], rsem.at[c], at_place(off, d))

                if OFFSETS[HOME][m] == 0 and d == 0:
                    if not isinstance(c, int):
                        pl.when(c != HOME)(far)
                    elif c != HOME:
                        far()
                else:
                    far()

    def send_fifth(src, dst, ssem, rsem, sign):
        for place, off in enumerate(ALL):
            if off != 0:
                rows = slice(16 * place, 16 * place + 16)
                to = at_place(off if sign > 0 else NZ - off, 0)
                send(src.at[FIFTH, rows, :], dst.at[FIFTH, rows, :], ssem.at[FIFTH], rsem.at[FIFTH], to)

    send_tiles(zout, zin, z_send, z_recv, MAIN[0], 1)

    for d in (2, 3, 1):
        send(meta.at[0], meta.at[d], meta_send, meta_recv, at_place(0, d))
    send(tok.at[0], tok.at[2], tok_send, tok_recv.at[1], at_place(0, 2))
    send(tok.at[0], tok.at[1], tok_send, tok_recv.at[0], at_place(0, 1))
    for c in MAIN[1:]:
        build(c)
        send_tiles(zout, zin, z_send, z_recv, c, 1)
    zin[HOME, OWN_TILE, :] = zout[HOME, OWN_TILE, :]

    def hand_on():
        wait(tok.at[2], tok_recv.at[1])
        send(tok.at[2], tok.at[3], tok_send, tok_recv.at[2], at_place(0, 1))

    def spread(part, to_blocks):
        if not to_blocks:
            return spreads[part]
        r, t = iota((ROWS, 4 * ROWS), 0), iota((ROWS, 4 * ROWS), 1)
        return (t == 16 * (r & 15) + 4 * part + (r >> 4)).astype(F32).astype(BF16)

    def to_tiles(rows):
        tiles = None
        for part in range(4):
            one = dot(spread(part, False), rows[:, 128 * part : 128 * part + 128], (0, 0))
            tiles = one if part == 0 else tiles + one
        return tiles.astype(BF16)

    def send_fifth_rows():
        wait(meta.at[1:NJ], meta_recv)
        wait(tok.at[1], tok_recv.at[0])
        wait(tok.at[3], tok_recv.at[2])
        r = iota((ROWS, 1), 0)
        code = code_of(choose(r >> 2, ALL), jnp.zeros_like(r), jnp.full_like(r, 4))
        rows = weight = None
        for d in range(NJ):
            hit, w = pick(jnp.where((r & 3) == d, code, -1.0), d)
            one = dot(hit.astype(BF16), tok[d], (1, 0))
            rows = one if d == 0 else rows + one
            weight = w if d == 0 else weight + w
        lanes = iota((1, 2 * WIDTH), 1)
        tiles = to_tiles(jnp.where(lanes < WIDTH, rows, weight * rows).astype(BF16))
        zout[FIFTH] = tiles
        zin[FIFTH, OWN_FIFTH, :] = tiles[OWN_FIFTH, :]
        send_fifth(zout, zin, z_send, z_recv, 1)

    for ro in range(1, reps):
        to = rid(ro // 2, ro % 2)
        rows = pl.ds(pl.multiple_of(to * share, 16), share)
        send(tok.at[0, rows, 0:WIDTH], hx.at[rep], hx_send, hx_recv, at(ro // 2, ro % 2))
    hx[rep] = tok[0, pl.ds(pl.multiple_of(rep * share, 16), share), 0:WIDTH]

    for copy in weights:
        copy.wait()

    low, high = slice(0, ROWS // 2), slice(ROWS // 2, ROWS)

    def gather(c):
        mine = gat.at[c, rep]
        send(mine, mine, c_send.at[c], c_recv.at[c, 0], at(0, 1))
        send(mine, mine, c_send.at[c], c_recv.at[c, 1], at(1, 0))
        send(mine, mine, c_send.at[c], c_recv.at[c, 2], at(-1, 0))

    def wait_tiles(ref, sem, c):
        fewer = (c == HOME) | (c == FIFTH)

        @pl.when(fewer)
        def _():
            wait(ref.at[c, 0:240, :], sem.at[c])

        @pl.when(jnp.logical_not(fewer))
        def _():
            wait(ref.at[c], sem.at[c])

    def stage_0(c):
        wait_tiles(zin, z_recv, c)
        tiles = zin[c]
        for part in range(4):
            cols = slice(128 * part, 128 * part + 128)
            gat[c, rep, :, cols] = dot(spread(part, False), tiles, (1, 0)).astype(BF16)
        gather(c)

    def stage_1(c):
        other, left, right = gat.at[c, rid(0, 1)], gat.at[c, rid(-1, 0)], gat.at[c, rid(1, 0)]
        wait(other, c_recv.at[c, 0])
        send(other, other, c_send.at[c], c_recv.at[c, 3], at(1, 0))
        send(other, other, c_send.at[c], c_recv.at[c, 4], at(-1, 0))
        wait(left, c_recv.at[c, 1])
        send(left.at[low, :], left.at[low, :], c_send.at[c], c_recv.at[c, 5], at(1, 0))
        wait(right, c_recv.at[c, 2])
        send(right.at[high, :], right.at[high, :], c_send.at[c], c_recv.at[c, 6], at(-1, 0))

    def stage_2(c):
        far = gat.at[c, rid(2, 0)]
        wait(far.at[low, :], c_recv.at[c, 5])
        wait(far.at[high, :], c_recv.at[c, 6])
        send(far, far, c_send.at[c], c_recv.at[c, 7], at(0, 1))

    def stage_3(c):
        wait(gat.at[c, rid(-1, 1)], c_recv.at[c, 3])
        wait(gat.at[c, rid(1, 1)], c_recv.at[c, 4])
        wait(gat.at[c, rid(2, 1)], c_recv.at[c, 7])
        squares = None
        for s in range(reps):
            v = gat[c, s, :, 0:WIDTH].astype(F32)
            part = jnp.sum(v * v, axis=1, keepdims=True)
            squares = part if s == 0 else squares + part
        scale = 1.0 / jnp.sqrt(squares / features + EPSILON)
        hidden_grad = None
        for s in range(reps):
            cols = slice(WIDTH * s, WIDTH * s + WIDTH)
            v = gat[c, s, :, 0:WIDTH].astype(F32)
            nrm[c, :, cols] = (v * gain_ref[:, cols] * scale).astype(BF16)
            part = dot(gat[c, s, :, WIDTH : 2 * WIDTH], wd[:, cols], (1, 1))
            hidden_grad = part if s == 0 else hidden_grad + part
        gate_pre = dot(nrm[c], wg[...], (1, 1))
        up_pre = dot(nrm[c], wu[...], (1, 1))
        sig = jax.nn.sigmoid(gate_pre)
        activated = gate_pre * sig
        hidden = (activated * up_pre).astype(BF16)
        gate_grad = (hidden_grad * up_pre * sig * (1.0 + gate_pre * (1.0 - sig))).astype(BF16)
        up_grad = (hidden_grad * activated).astype(BF16)
        hid[c], ggr[c], ugr[c] = hidden, gate_grad, up_grad
        for s in range(reps):
            cols = slice(WIDTH * s, WIDTH * s + WIDTH)
            par[c, s, :, 0:WIDTH] = dot(hidden, wd[:, cols], (1, 0)).astype(BF16)
            par[c, s, :, WIDTH : 2 * WIDTH] = (
                dot(gate_grad, wg[:, cols], (1, 0)) + dot(up_grad, wu[:, cols], (1, 0))
            ).astype(BF16)
        send(par.at[c, rid(2, 1)], got.at[c, 0], e_send.at[c], e_recv.at[c, 0], at(0, 1))
        send(par.at[c, rid(1, 1)], got.at[c, 1], e_send.at[c], e_recv.at[c, 1], at(1, 0))
        send(par.at[c, rid(-1, 1)], got.at[c, 2], e_send.at[c], e_recv.at[c, 2], at(-1, 0))

    def stage_4(c):
        far, other = rid(2, 0), rid(0, 1)
        wait(got.at[c, 0], e_recv.at[c, 0])
        par[c, far] = (par[c, far].astype(F32) + got[c, 0].astype(F32)).astype(BF16)
        send(par.at[c, far, low, :], got.at[c, 3, low, :], e_send.at[c], e_recv.at[c, 3], at(1, 0))
        send(par.at[c, far, high, :], got.at[c, 3, high, :], e_send.at[c], e_recv.at[c, 7], at(-1, 0))
        wait(got.at[c, 1], e_recv.at[c, 1])
        wait(got.at[c, 2], e_recv.at[c, 2])
        par[c, other] = (
            par[c, other].astype(F32) + got[c, 1].astype(F32) + got[c, 2].astype(F32)
        ).astype(BF16)
        send(par.at[c, other], got.at[c, 6], e_send.at[c], e_recv.at[c, 6], at(0, 1))

    def stage_5(c):
        right, left = rid(1, 0), rid(-1, 0)
        wait(got.at[c, 3, low, :], e_recv.at[c, 3])
        par[c, right, low, :] = (par[c, right, low, :].astype(F32) + got[c, 3, low, :].astype(F32)).astype(BF16)
        send(par.at[c, right], got.at[c, 4], e_send.at[c], e_recv.at[c, 4], at(1, 0))
        wait(got.at[c, 3, high, :], e_recv.at[c, 7])
        par[c, left, high, :] = (par[c, left, high, :].astype(F32) + got[c, 3, high, :].astype(F32)).astype(BF16)
        send(par.at[c, left], got.at[c, 5], e_send.at[c], e_recv.at[c, 5], at(-1, 0))

    def stage_6(c):
        total = par[c, rep].astype(F32)
        for k in (6, 4, 5):
            wait(got.at[c, k], e_recv.at[c, k])
            total = total + got[c, k].astype(F32)
        tiles = to_tiles(total.astype(BF16))
        fout[c] = tiles

        @pl.when(c != FIFTH)
        def _():
            send_tiles(fout, fback, f_send, f_recv, c, -1)

        @pl.when(c == HOME)
        def _():
            fback[HOME, OWN_TILE, :] = tiles[OWN_TILE, :]

        @pl.when(c == FIFTH)
        def _():
            fback[FIFTH, OWN_FIFTH, :] = tiles[OWN_FIFTH, :]
            send_fifth(fout, fback, f_send, f_recv, -1)

    def add_rows(code, rows):
        for k in range(2):
            one = (code == meta[0, k : k + 1, :]).astype(F32).astype(BF16)
            picked[k] = picked[k] + dot(one, rows, (0, 0))

    def stage_7(c):
        wait_tiles(fback, f_recv, c)
        tiles = fback[c]

        @pl.when(c != FIFTH)
        def _():
            rows = [dot(spread(part, False), tiles, (1, 0)).astype(BF16) for part in range(4)]
            r = iota((ROWS, 1), 0)
            code = code_of(choose(r >> 4, [z_offset(c, m) for m in range(4)]), (r >> 2) & 3, r & 3)
            add_rows(code, jnp.concatenate(rows, axis=1))

        @pl.when(c == FIFTH)
        def _():
            for part in range(4):
                cols = slice(128 * part, 128 * part + 128)
                rows = dot(spread(part, True), tiles, (1, 0)).astype(BF16)
                fifth_in[0:16, cols] = rows[0:16, :]
                for d in range(1, NJ):
                    loc[d, :, cols] = rows[16 * d : 16 * d + 16, :]
            for d in range(1, NJ):
                rows = slice(16 * d, 16 * d + 16)
                send(loc.at[d], fifth_in.at[rows, :], l_send, l_recv, at_place(0, d))

    def turned(ref):
        return jnp.transpose(ref[...].reshape(CHUNKS * ROWS, ref.shape[2]).astype(F32)).astype(BF16)

    def update(s):
        cols = pl.ds(pl.multiple_of(s * WIDTH, WIDTH), WIDTH)
        rows_n = nrm[:, :, cols].reshape(CHUNKS * ROWS, WIDTH)
        rows_g = gat[:, s, :, WIDTH : 2 * WIDTH].reshape(CHUNKS * ROWS, WIDTH)
        gu[:, cols] = dot(ggt[...], rows_n, (1, 0)).astype(BF16)
        uu[:, cols] = dot(ugt[...], rows_n, (1, 0)).astype(BF16)
        du[:, cols] = dot(ht[...], rows_g, (1, 0)).astype(BF16)

    stages = (
        (9, stage_7), (6, stage_6), (5, stage_5), (4, stage_4), (3, stage_3), (2, stage_2), (1, stage_1), (0, stage_0)
    )
    first_free = CHUNKS + 6
    ticks = CHUNKS + stages[0][0]
    per_tick = reps // 2

    def tick(t, carry):
        for lag, stage in reversed(stages):
            pl.when((t >= lag) & (t - lag < CHUNKS))(functools.partial(stage, t - lag))

        @pl.when(t == first_free)
        def _():
            ht[...], ggt[...], ugt[...] = turned(hid), turned(ggr), turned(ugr)

        @pl.when((t >= first_free) & (t < first_free + reps // per_tick))
        def _():
            for s in range(per_tick):
                update((t - first_free) * per_tick + s)

        return carry

    picked[...] = jnp.zeros_like(picked)
    hand_on()
    send_fifth_rows()
    diagonal = iota((128, 128), 0) == iota((128, 128), 1)
    w = [jnp.sum(jnp.where(diagonal, meta[0, 2 + k : 3 + k, :], 0.0), axis=1, keepdims=True) for k in range(2)]
    wait(hx.at[pl.ds(0, reps - 1)], hx_recv)
    squares = None
    for s in range(reps):
        v = hx[s].astype(F32)
        part = jnp.sum(v * v, axis=1, keepdims=True)
        squares = part if s == 0 else squares + part
    root = jnp.sqrt(squares / features + EPSILON)
    lax.fori_loop(0, ticks, tick, 0)

    updates = [
        pltpu.make_async_copy(gu, gu_out, o_sem.at[0]),
        pltpu.make_async_copy(uu, uu_out, o_sem.at[1]),
        pltpu.make_async_copy(du, du_out, o_sem.at[2]),
    ]
    for copy in updates:
        copy.start()

    grad = tok[0, :, WIDTH:].astype(F32)

    r = iota((ROWS, 1), 0)
    code = code_of(choose(r & 15, ALL), r >> 4, jnp.full_like(r, 4))
    wait(fifth_in.at[16:64, :], l_recv)
    add_rows(code, fifth_in[...])
    out_rows = [picked[k, :, 0:WIDTH] for k in range(2)]
    share_out = (w[0] * out_rows[0] + w[1] * out_rows[1]).astype(BF16)
    share_in = (picked[0, :, WIDTH:] + picked[1, :, WIDTH:]).astype(BF16)
    dots = [jnp.sum(p * grad, axis=1, keepdims=True) for p in out_rows]
    heads = [d.astype(BF16).astype(F32) for d in dots]
    lane = iota((128, 128), 1)
    products = jnp.where(
        lane == 0, heads[0],
        jnp.where(lane == 1, heads[1], jnp.where(lane == 2, dots[0] - heads[0], jnp.where(lane == 3, dots[1] - heads[1], 0.0))),
    ).astype(BF16)
    halves = [share_out[:, 0:128], share_out[:, 128:], share_in[:, 0:128], share_in[:, 128:], products]
    for s in range(reps):
        for i, half in enumerate(halves):
            fin[s, share * i : share * i + share, :] = half[share * s : share * s + share, :]
    for ro in range(1, reps):
        send(fin.at[rid(ro // 2, ro % 2)], fin_in.at[rep], y_send, y_recv, at(ro // 2, ro % 2))
    fin_in[rep] = fin[rep]

    wait(fin_in.at[pl.ds(0, reps - 1)], y_recv)
    inner = route = None
    for s in range(2 * reps):
        cols = slice(128 * s, 128 * s + 128)
        v = hx[s // 2, :, 128 * (s % 2) : 128 * (s % 2) + 128].astype(F32)
        at_out, at_in = share * (s % 2), share * (2 + s % 2)
        lo_ref[:, cols] = (v + fin_in[s // 2, at_out : at_out + share, :].astype(F32)).astype(BF16)
        scaled = gain_ref[:, cols] * fin_in[s // 2, at_in : at_in + share, :].astype(F32)
        part = jnp.sum(scaled * v, axis=1, keepdims=True)
        inner = part if s == 0 else inner + part
    for s in range(reps):
        part = fin_in[s, 4 * share :, :].astype(F32)
        route = part if s == 0 else route + part
    coefficient = inner / (features * root * root * root)
    for s in range(2 * reps):
        cols = slice(128 * s, 128 * s + 128)
        v = hx[s // 2, :, 128 * (s % 2) : 128 * (s % 2) + 128].astype(F32)
        at_in = share * (2 + s % 2)
        scaled = gain_ref[:, cols] * fin_in[s // 2, at_in : at_in + share, :].astype(F32)
        ig_ref[:, cols] = (scaled / root - v * coefficient).astype(BF16)
    diagonal = iota((share, share), 0) == iota((share, share), 1)
    for k in range(2):
        column = route[:, k : k + 1] + route[:, 2 + k : 3 + k]
        rg_ref[k : k + 1, :] = jnp.sum(jnp.where(diagonal, column, 0.0), axis=0, keepdims=True)

    wait(meta.at[1:NJ], meta_send)
    wait(tok.at[1:NJ], tok_send)
    wait(hx.at[pl.ds(0, reps - 1)], hx_send)
    for c in range(CHUNKS):
        sent = slice(0, 240 if c in (HOME, FIFTH) else 256)
        wait(zout.at[c, sent, :], z_send.at[c])
        wait(fout.at[c, sent, :], f_send.at[c])
    for c in range(CHUNKS):
        wait(gat.at[c, pl.ds(0, 7)], c_send.at[c])
        wait(got.at[c], e_send.at[c])
    wait(loc.at[1:NJ], l_send)
    wait(fin.at[pl.ds(0, reps - 1)], y_send)
    for copy in updates:
        copy.wait()


def hand_out(*refs):
    n = (len(refs) - 2) // 3
    sources, results, held, in_sem, out_sem = refs[:n], refs[n : 2 * n], refs[2 * n : 3 * n], refs[-2], refs[-1]
    pieces = [(i, slice(96 * k, 96 * k + 96)) for i in range(3, n) for k in range(2)]
    pieces += [(i, slice(None)) for i in range(3)]
    arriving, leaving = [], []
    for k, (i, rows) in enumerate(pieces):
        arriving.append(pltpu.make_async_copy(sources[i].at[rows, :], held[i].at[rows, :], in_sem.at[k]))
        arriving[-1].start()
    for k, (i, rows) in enumerate(pieces):
        arriving[k].wait()
        leaving.append(pltpu.make_async_copy(held[i].at[rows, :], results[i].at[rows, :], out_sem.at[k]))
        leaving[-1].start()
    for copy in leaving:
        copy.wait()


def body(hidden_in, norm_gain, route_ids, route_weights, w_gate, w_up, w_down, out_grad):
    reps = lax.axis_size("rep")
    units, features = w_gate.shape[1:]
    tokens = hidden_in.shape[0]
    share = tokens // reps
    vmem = pl.BlockSpec(memory_space=pltpu.VMEM)
    hbm = pl.BlockSpec(memory_space=pltpu.HBM)
    anywhere = pl.BlockSpec(memory_space=pl.ANY)
    matrix = pltpu.VMEM((units, features), BF16)
    dma = pltpu.SemaphoreType.DMA
    rows = CHUNKS * ROWS
    scratch = [matrix] * 6 + [
        pltpu.VMEM((2, tokens), jnp.int32),
        pltpu.VMEM((2, tokens), F32),
        pltpu.VMEM((1, features), F32),
        pltpu.VMEM((4, ROWS, 4 * ROWS), BF16),
        pltpu.VMEM((NJ, tokens, 2 * WIDTH), BF16),
        pltpu.VMEM((NJ, 8, tokens), F32),
        pltpu.VMEM((reps, share, WIDTH), BF16),
        pltpu.VMEM((CHUNKS, 4 * ROWS, 128), BF16),
        pltpu.VMEM((CHUNKS, 4 * ROWS, 128), BF16),
        pltpu.VMEM((CHUNKS, reps, ROWS, 2 * WIDTH), BF16),
        pltpu.VMEM((CHUNKS, ROWS, features), BF16),
        pltpu.VMEM((CHUNKS, reps, ROWS, 2 * WIDTH), BF16),
        pltpu.VMEM((CHUNKS, 7, ROWS, 2 * WIDTH), BF16),
        pltpu.VMEM((CHUNKS, 4 * ROWS, 128), BF16),
        pltpu.VMEM((CHUNKS, 4 * ROWS, 128), BF16),
        pltpu.VMEM((NJ, 16, 2 * WIDTH), BF16),
        pltpu.VMEM((ROWS, 2 * WIDTH), BF16),
        pltpu.VMEM((2, tokens, 2 * WIDTH), F32),
        pltpu.VMEM((reps, 5 * share, 128), BF16),
        pltpu.VMEM((reps, 5 * share, 128), BF16),
    ]
    scratch += [pltpu.VMEM((CHUNKS, ROWS, units), BF16)] * 3
    scratch += [pltpu.VMEM((units, rows), BF16)] * 3
    scratch += [
        dma((3,)), dma((3,)), dma((5,)),
        dma, dma, dma, dma((3,)),
        dma, dma,
        dma((CHUNKS,)), dma((CHUNKS,)),
        dma((CHUNKS,)), dma((CHUNKS, 8)),
        dma((CHUNKS,)), dma((CHUNKS, 8)),
        dma((CHUNKS,)), dma((CHUNKS,)),
        dma, dma,
        dma, dma,
    ]
    update = jax.ShapeDtypeStruct((units, features), BF16)
    kinds = (
        jax.ShapeDtypeStruct((share, features), BF16),
        jax.ShapeDtypeStruct((share, features), BF16),
        jax.ShapeDtypeStruct((2, share), F32),
        update, update, update,
    )
    outs = pl.pallas_call(
        kernel,
        out_shape=kinds,
        in_specs=[hbm] * 8,
        out_specs=(vmem, vmem, vmem, anywhere, anywhere, anywhere),
        scratch_shapes=scratch,
        compiler_params=pltpu.CompilerParams(
            collective_id=0, has_side_effects=True, vmem_limit_bytes=62 * 1024 * 1024
        ),
        name="expert_layer",
    )(
        hidden_in, out_grad, route_ids.T, route_weights.T, norm_gain[None, :], w_gate[0], w_up[0], w_down[0]
    )
    outs = pl.pallas_call(
        hand_out,
        out_shape=kinds,
        in_specs=[anywhere] * 6,
        out_specs=(anywhere,) * 6,
        scratch_shapes=[pltpu.VMEM(kind.shape, kind.dtype) for kind in kinds] + [dma((9,)), dma((9,))],
        name="results",
    )(*outs)
    layer_out, input_grad, route_grad, gate_update, up_update, down_update = outs
    return layer_out, input_grad, route_grad.T, gate_update[None], up_update[None], down_update[None]


def solution(mesh):
    placed = (
        P("exp", "rep"),
        P(),
        P("exp", None),
        P("exp", None),
        P("exp", "rep", None),
        P("exp", "rep", None),
        P("exp", "rep", None),
        P("exp", "rep"),
    )
    return jax.shard_map(
        body,
        mesh=mesh,
        in_specs=placed,
        out_specs=(
            P(("exp", "rep"), None),
            P(("exp", "rep"), None),
            P(("exp", "rep"), None),
            P("exp", "rep", None),
            P("exp", "rep", None),
            P("exp", "rep", None),
        ),
        check_vma=False,
    )
```

```python
import functools

import jax
import jax.numpy as jnp
from jax import lax
from jax.experimental import pallas as pl
from jax.experimental.pallas import tpu as pltpu
from jax.sharding import PartitionSpec as P

LOGICAL = pl.DeviceIdType.LOGICAL
EPSILON = 1e-06
NZ = 16
NJ = 4
WIDTH = 256
CHUNKS = 5
ROWS = 64
F32 = jnp.float32
BF16 = jnp.bfloat16


OFFSETS = ((0, 3, 13, 4), (7, 9, 8, 10), None, (5, 11, 6, 12), (1, 2, 14, 15))
FIFTH = OFFSETS.index(None)
MAIN = tuple(c for c in range(CHUNKS) if c != FIFTH)
ALL = sum((OFFSETS[c] for c in MAIN), ())
HOME = next(c for c in MAIN if 0 in OFFSETS[c])
OWN_TILE = slice(64 * OFFSETS[HOME].index(0), 64 * OFFSETS[HOME].index(0) + 16)
OWN_FIFTH = slice(16 * ALL.index(0), 16 * ALL.index(0) + 16)


def choose(index, values):
    out = jnp.full_like(index, values[0])
    for i in range(1, len(values)):
        out = jnp.where(index == i, values[i], out)
    return out


def z_offset(c, m):
    if isinstance(c, int):
        return OFFSETS[c][m]
    return choose(c, [OFFSETS[i][m] if i != FIFTH else 0 for i in range(CHUNKS)])


def iota(shape, dim):
    return lax.broadcasted_iota(jnp.int32, shape, dim)


def dot(a, b, dims):
    return lax.dot_general(a, b, ((dims[:1], dims[1:]), ((), ())), preferred_element_type=F32)


def kernel(
    h_hbm, g_hbm, ids_hbm, wrow_hbm, gain_hbm, wg_hbm, wu_hbm, wd_hbm,
    lo_ref, ig_ref, rg_ref, gu_out, uu_out, du_out,
    wg, wu, wd, gu, uu, du,
    ids_ref, wrow_ref, gain_ref, spreads, tok, meta, hx, zout, zin, gat, nrm, par, got, fout, fback, loc, fifth_in, picked, fin, fin_in,
    hid, ggr, ugr, ht, ggt, ugt,
    w_sem, o_sem, own_sem, meta_send, meta_recv, tok_send, tok_recv, hx_send, hx_recv,
    z_send, z_recv, c_send, c_recv, e_send, e_recv, f_send, f_recv, l_send, l_recv, y_send, y_recv,
):
    reps = lax.axis_size("rep")
    features = reps * WIDTH
    share = h_hbm.shape[0] // reps
    rep = lax.axis_index("rep")
    exp = lax.axis_index("exp")
    z, j = exp // NJ, exp % NJ
    columns = reps // 2
    x, y = rep // 2, rep % 2

    here = rep * (NZ * NJ)
    planes = [lax.rem(j // 2 + d // 2, 2) * 2 + lax.rem(j % 2 + d % 2, 2) for d in range(NJ)]
    ids_z = [here + lax.rem(z + off, NZ) * NJ for off in range(NZ)]
    slots = {
        (dx, dy): lax.rem(x + columns + dx, columns) * 2 + lax.rem(y + dy, 2) for dx in (-1, 0, 1, 2) for dy in (0, 1)
    }

    def in_plane(d):
        return planes[d]

    def at_place(off, d):
        if isinstance(off, int):
            return ids_z[off % NZ] + planes[d]
        return here + lax.rem(z + off, NZ) * NJ + planes[d]

    def rid(dx, dy):
        return slots[(dx + 1) % columns - 1, dy]

    def at(dx, dy):
        return rid(dx, dy) * (NZ * NJ) + exp

    def send(src, dst, ssem, rsem, device):
        pltpu.make_async_remote_copy(
            src_ref=src, dst_ref=dst, send_sem=ssem, recv_sem=rsem, device_id=device, device_id_type=LOGICAL
        ).start()

    def wait(ref, sem):
        pltpu.make_async_copy(ref, ref, sem).wait()

    routes = [
        pltpu.make_async_copy(ids_hbm, ids_ref, own_sem.at[2]),
        pltpu.make_async_copy(wrow_hbm, wrow_ref, own_sem.at[3]),
        pltpu.make_async_copy(gain_hbm, gain_ref, own_sem.at[4]),
    ]
    own = [
        pltpu.make_async_copy(h_hbm, tok.at[0, :, 0:WIDTH], own_sem.at[0]),
        pltpu.make_async_copy(g_hbm, tok.at[0, :, WIDTH : 2 * WIDTH], own_sem.at[1]),
    ]
    weights = [
        pltpu.make_async_copy(wg_hbm, wg, w_sem.at[0]),
        pltpu.make_async_copy(wu_hbm, wu, w_sem.at[1]),
        pltpu.make_async_copy(wd_hbm, wd, w_sem.at[2]),
    ]
    for copy in routes + own + weights:
        copy.start()

    barrier = pltpu.get_barrier_semaphore()

    for off in sorted(range(NZ), key=lambda off: -min(off, NZ - off)):
        for d in range(NJ):
            if off or d:
                pl.semaphore_signal(barrier, inc=1, device_id=at_place(off, d), device_id_type=LOGICAL)
    for ro in range(1, reps):
        pl.semaphore_signal(barrier, inc=1, device_id=at(ro // 2, ro % 2), device_id_type=LOGICAL)

    for copy in routes:
        copy.wait()
    ids = ids_ref[...]
    expert_rows = iota((NZ * NJ, 128), 0)
    hits = [(expert_rows == ids[k : k + 1, :]).astype(F32) for k in range(2)]
    before = (iota((128, 128), 0) < iota((128, 128), 1)).astype(F32).astype(BF16)
    earlier = dot((hits[0] + hits[1]).astype(BF16), before, (1, 0))
    for k in range(2):
        number = jnp.sum(hits[k] * earlier, axis=0, keepdims=True)
        meta[0, k : k + 1, :] = ids[k : k + 1, :].astype(F32) * 8.0 + number
    meta[0, 2:4, :] = wrow_ref[...]
    meta[0, 4:8, :] = jnp.zeros((4, 128), F32)

    for copy in own:
        copy.wait()

    def code_of(off, place, number):
        plane = (z + off) & (NZ - 1)
        return ((plane * NJ + choose(place, [in_plane(d) for d in range(NJ)])) * 8 + number).astype(F32)

    r = iota((4 * ROWS, 1), 0)
    part_of = (r >> 2) & 3
    blocks = jnp.concatenate([tok[0, :, 128 * f : 128 * f + 128] for f in range(4)], axis=0)

    def pick(code, d):
        one = [code == meta[d, k : k + 1, :] for k in range(2)]
        w = jnp.where(one[0], meta[d, 2:3, :], 0.0) + jnp.where(one[1], meta[d, 3:4, :], 0.0)
        return (one[0] | one[1]).astype(F32), jnp.sum(w, axis=1, keepdims=True)

    def build(c):
        hit, weight = pick(code_of(choose(r >> 6, OFFSETS[c]), (r >> 4) & 3, r & 3), 0)
        masks = jnp.concatenate([jnp.where(part_of == f, hit, 0.0) for f in range(4)], axis=1).astype(BF16)
        tiles = dot(masks, blocks, (1, 0))
        zout[c] = jnp.where(part_of >= 2, weight * tiles, tiles).astype(BF16)

    build(MAIN[0])
    row, col = iota((ROWS, 4 * ROWS), 0), iota((ROWS, 4 * ROWS), 1)
    for part in range(4):
        spreads[part] = (col == 16 * (row >> 2) + 4 * part + (row & 3)).astype(F32).astype(BF16)
    pl.semaphore_wait(barrier, NZ * NJ - 1 + reps - 1)

    def send_tiles(src, dst, ssem, rsem, c, sign):
        for m in range(4):
            off = z_offset(c, m)
            off = off if sign > 0 else NZ - off
            for d in range(NJ):
                rows = slice(64 * m + 16 * d, 64 * m + 16 * d + 16)

                def far(rows=rows, d=d, off=off):
                    send(src.at[c, rows, :], dst.at[c, rows, :], ssem.at[c], rsem.at[c], at_place(off, d))

                if OFFSETS[HOME][m] == 0 and d == 0:
                    if not isinstance(c, int):
                        pl.when(c != HOME)(far)
                    elif c != HOME:
                        far()
                else:
                    far()

    def send_fifth(src, dst, ssem, rsem, sign):
        for place, off in enumerate(ALL):
            if off != 0:
                rows = slice(16 * place, 16 * place + 16)
                to = at_place(off if sign > 0 else NZ - off, 0)
                send(src.at[FIFTH, rows, :], dst.at[FIFTH, rows, :], ssem.at[FIFTH], rsem.at[FIFTH], to)

    send_tiles(zout, zin, z_send, z_recv, MAIN[0], 1)

    for d in (2, 3, 1):
        send(meta.at[0], meta.at[d], meta_send, meta_recv, at_place(0, d))
    send(tok.at[0], tok.at[2], tok_send, tok_recv.at[1], at_place(0, 2))
    send(tok.at[0], tok.at[1], tok_send, tok_recv.at[0], at_place(0, 1))
    for c in MAIN[1:]:
        build(c)
        send_tiles(zout, zin, z_send, z_recv, c, 1)
    zin[HOME, OWN_TILE, :] = zout[HOME, OWN_TILE, :]

    def hand_on():
        wait(tok.at[2], tok_recv.at[1])
        send(tok.at[2], tok.at[3], tok_send, tok_recv.at[2], at_place(0, 1))

    def spread(part, to_blocks):
        if not to_blocks:
            return spreads[part]
        r, t = iota((ROWS, 4 * ROWS), 0), iota((ROWS, 4 * ROWS), 1)
        return (t == 16 * (r & 15) + 4 * part + (r >> 4)).astype(F32).astype(BF16)

    def to_tiles(rows):
        tiles = None
        for part in range(4):
            one = dot(spread(part, False), rows[:, 128 * part : 128 * part + 128], (0, 0))
            tiles = one if part == 0 else tiles + one
        return tiles.astype(BF16)

    def send_fifth_rows():
        wait(meta.at[1:NJ], meta_recv)
        wait(tok.at[1], tok_recv.at[0])
        wait(tok.at[3], tok_recv.at[2])
        r = iota((ROWS, 1), 0)
        code = code_of(choose(r >> 2, ALL), jnp.zeros_like(r), jnp.full_like(r, 4))
        rows = weight = None
        for d in range(NJ):
            hit, w = pick(jnp.where((r & 3) == d, code, -1.0), d)
            one = dot(hit.astype(BF16), tok[d], (1, 0))
            rows = one if d == 0 else rows + one
            weight = w if d == 0 else weight + w
        lanes = iota((1, 2 * WIDTH), 1)
        tiles = to_tiles(jnp.where(lanes < WIDTH, rows, weight * rows).astype(BF16))
        zout[FIFTH] = tiles
        zin[FIFTH, OWN_FIFTH, :] = tiles[OWN_FIFTH, :]
        send_fifth(zout, zin, z_send, z_recv, 1)

    for ro in range(1, reps):
        to = rid(ro // 2, ro % 2)
        rows = pl.ds(pl.multiple_of(to * share, 16), share)
        send(tok.at[0, rows, 0:WIDTH], hx.at[rep], hx_send, hx_recv, at(ro // 2, ro % 2))
    hx[rep] = tok[0, pl.ds(pl.multiple_of(rep * share, 16), share), 0:WIDTH]

    for copy in weights:
        copy.wait()

    low, high = slice(0, ROWS // 2), slice(ROWS // 2, ROWS)

    def gather(c):
        mine = gat.at[c, rep]
        send(mine, mine, c_send.at[c], c_recv.at[c, 0], at(0, 1))
        send(mine, mine, c_send.at[c], c_recv.at[c, 1], at(1, 0))
        send(mine, mine, c_send.at[c], c_recv.at[c, 2], at(-1, 0))

    def wait_tiles(ref, sem, c):
        fewer = (c == HOME) | (c == FIFTH)

        @pl.when(fewer)
        def _():
            wait(ref.at[c, 0:240, :], sem.at[c])

        @pl.when(jnp.logical_not(fewer))
        def _():
            wait(ref.at[c], sem.at[c])

    def stage_0(c):
        wait_tiles(zin, z_recv, c)
        tiles = zin[c]
        for part in range(4):
            cols = slice(128 * part, 128 * part + 128)
            gat[c, rep, :, cols] = dot(spread(part, False), tiles, (1, 0)).astype(BF16)
        gather(c)

    def stage_1(c):
        other, left, right = gat.at[c, rid(0, 1)], gat.at[c, rid(-1, 0)], gat.at[c, rid(1, 0)]
        wait(other, c_recv.at[c, 0])
        send(other, other, c_send.at[c], c_recv.at[c, 3], at(1, 0))
        send(other, other, c_send.at[c], c_recv.at[c, 4], at(-1, 0))
        wait(left, c_recv.at[c, 1])
        send(left.at[low, :], left.at[low, :], c_send.at[c], c_recv.at[c, 5], at(1, 0))
        wait(right, c_recv.at[c, 2])
        send(right.at[high, :], right.at[high, :], c_send.at[c], c_recv.at[c, 6], at(-1, 0))

    def stage_2(c):
        far = gat.at[c, rid(2, 0)]
        wait(far.at[low, :], c_recv.at[c, 5])
        wait(far.at[high, :], c_recv.at[c, 6])
        send(far, far, c_send.at[c], c_recv.at[c, 7], at(0, 1))

    def stage_3(c):
        wait(gat.at[c, rid(-1, 1)], c_recv.at[c, 3])
        wait(gat.at[c, rid(1, 1)], c_recv.at[c, 4])
        wait(gat.at[c, rid(2, 1)], c_recv.at[c, 7])
        squares = None
        for s in range(reps):
            v = gat[c, s, :, 0:WIDTH].astype(F32)
            part = jnp.sum(v * v, axis=1, keepdims=True)
            squares = part if s == 0 else squares + part
        scale = 1.0 / jnp.sqrt(squares / features + EPSILON)
        hidden_grad = None
        for s in range(reps):
            cols = slice(WIDTH * s, WIDTH * s + WIDTH)
            v = gat[c, s, :, 0:WIDTH].astype(F32)
            nrm[c, :, cols] = (v * gain_ref[:, cols] * scale).astype(BF16)
            part = dot(gat[c, s, :, WIDTH : 2 * WIDTH], wd[:, cols], (1, 1))
            hidden_grad = part if s == 0 else hidden_grad + part
        gate_pre = dot(nrm[c], wg[...], (1, 1))
        up_pre = dot(nrm[c], wu[...], (1, 1))
        sig = jax.nn.sigmoid(gate_pre)
        activated = gate_pre * sig
        hidden = (activated * up_pre).astype(BF16)
        gate_grad = (hidden_grad * up_pre * sig * (1.0 + gate_pre * (1.0 - sig))).astype(BF16)
        up_grad = (hidden_grad * activated).astype(BF16)
        hid[c], ggr[c], ugr[c] = hidden, gate_grad, up_grad
        for s in range(reps):
            cols = slice(WIDTH * s, WIDTH * s + WIDTH)
            par[c, s, :, 0:WIDTH] = dot(hidden, wd[:, cols], (1, 0)).astype(BF16)
            par[c, s, :, WIDTH : 2 * WIDTH] = (
                dot(gate_grad, wg[:, cols], (1, 0)) + dot(up_grad, wu[:, cols], (1, 0))
            ).astype(BF16)
        send(par.at[c, rid(2, 1)], got.at[c, 0], e_send.at[c], e_recv.at[c, 0], at(0, 1))
        send(par.at[c, rid(1, 1)], got.at[c, 1], e_send.at[c], e_recv.at[c, 1], at(1, 0))
        send(par.at[c, rid(-1, 1)], got.at[c, 2], e_send.at[c], e_recv.at[c, 2], at(-1, 0))

    def stage_4(c):
        far, other = rid(2, 0), rid(0, 1)
        wait(got.at[c, 0], e_recv.at[c, 0])
        par[c, far] = (par[c, far].astype(F32) + got[c, 0].astype(F32)).astype(BF16)
        send(par.at[c, far, low, :], got.at[c, 3, low, :], e_send.at[c], e_recv.at[c, 3], at(1, 0))
        send(par.at[c, far, high, :], got.at[c, 3, high, :], e_send.at[c], e_recv.at[c, 7], at(-1, 0))
        wait(got.at[c, 1], e_recv.at[c, 1])
        wait(got.at[c, 2], e_recv.at[c, 2])
        par[c, other] = (
            par[c, other].astype(F32) + got[c, 1].astype(F32) + got[c, 2].astype(F32)
        ).astype(BF16)
        send(par.at[c, other], got.at[c, 6], e_send.at[c], e_recv.at[c, 6], at(0, 1))

    def stage_5(c):
        right, left = rid(1, 0), rid(-1, 0)
        wait(got.at[c, 3, low, :], e_recv.at[c, 3])
        par[c, right, low, :] = (par[c, right, low, :].astype(F32) + got[c, 3, low, :].astype(F32)).astype(BF16)
        send(par.at[c, right], got.at[c, 4], e_send.at[c], e_recv.at[c, 4], at(1, 0))
        wait(got.at[c, 3, high, :], e_recv.at[c, 7])
        par[c, left, high, :] = (par[c, left, high, :].astype(F32) + got[c, 3, high, :].astype(F32)).astype(BF16)
        send(par.at[c, left], got.at[c, 5], e_send.at[c], e_recv.at[c, 5], at(-1, 0))

    def stage_6(c):
        total = par[c, rep].astype(F32)
        for k in (6, 4, 5):
            wait(got.at[c, k], e_recv.at[c, k])
            total = total + got[c, k].astype(F32)
        tiles = to_tiles(total.astype(BF16))
        fout[c] = tiles

        @pl.when(c != FIFTH)
        def _():
            send_tiles(fout, fback, f_send, f_recv, c, -1)

        @pl.when(c == HOME)
        def _():
            fback[HOME, OWN_TILE, :] = tiles[OWN_TILE, :]

        @pl.when(c == FIFTH)
        def _():
            fback[FIFTH, OWN_FIFTH, :] = tiles[OWN_FIFTH, :]
            send_fifth(fout, fback, f_send, f_recv, -1)

    def add_rows(code, rows):
        for k in range(2):
            one = (code == meta[0, k : k + 1, :]).astype(F32).astype(BF16)
            picked[k] = picked[k] + dot(one, rows, (0, 0))

    def stage_7(c):
        wait_tiles(fback, f_recv, c)
        tiles = fback[c]

        @pl.when(c != FIFTH)
        def _():
            rows = [dot(spread(part, False), tiles, (1, 0)).astype(BF16) for part in range(4)]
            r = iota((ROWS, 1), 0)
            code = code_of(choose(r >> 4, [z_offset(c, m) for m in range(4)]), (r >> 2) & 3, r & 3)
            add_rows(code, jnp.concatenate(rows, axis=1))

        @pl.when(c == FIFTH)
        def _():
            for part in range(4):
                cols = slice(128 * part, 128 * part + 128)
                rows = dot(spread(part, True), tiles, (1, 0)).astype(BF16)
                fifth_in[0:16, cols] = rows[0:16, :]
                for d in range(1, NJ):
                    loc[d, :, cols] = rows[16 * d : 16 * d + 16, :]
            for d in range(1, NJ):
                rows = slice(16 * d, 16 * d + 16)
                send(loc.at[d], fifth_in.at[rows, :], l_send, l_recv, at_place(0, d))

    def turned(ref):
        return jnp.transpose(ref[...].reshape(CHUNKS * ROWS, ref.shape[2]).astype(F32)).astype(BF16)

    def update(s):
        cols = pl.ds(pl.multiple_of(s * WIDTH, WIDTH), WIDTH)
        rows_n = nrm[:, :, cols].reshape(CHUNKS * ROWS, WIDTH)
        rows_g = gat[:, s, :, WIDTH : 2 * WIDTH].reshape(CHUNKS * ROWS, WIDTH)
        gu[:, cols] = dot(ggt[...], rows_n, (1, 0)).astype(BF16)
        uu[:, cols] = dot(ugt[...], rows_n, (1, 0)).astype(BF16)
        du[:, cols] = dot(ht[...], rows_g, (1, 0)).astype(BF16)

    stages = (
        (8, stage_7), (6, stage_6), (5, stage_5), (4, stage_4), (3, stage_3), (2, stage_2), (1, stage_1), (0, stage_0)
    )
    first_free = CHUNKS + 6
    ticks = CHUNKS + stages[0][0]
    per_tick = reps // 2

    def tick(t, carry):
        for lag, stage in reversed(stages):
            pl.when((t >= lag) & (t - lag < CHUNKS))(functools.partial(stage, t - lag))

        @pl.when(t == first_free)
        def _():
            ht[...], ggt[...], ugt[...] = turned(hid), turned(ggr), turned(ugr)

        @pl.when((t >= first_free) & (t < first_free + reps // per_tick))
        def _():
            for s in range(per_tick):
                update((t - first_free) * per_tick + s)

        return carry

    picked[...] = jnp.zeros_like(picked)
    hand_on()
    send_fifth_rows()
    diagonal = iota((128, 128), 0) == iota((128, 128), 1)
    w = [jnp.sum(jnp.where(diagonal, meta[0, 2 + k : 3 + k, :], 0.0), axis=1, keepdims=True) for k in range(2)]
    wait(hx.at[pl.ds(0, reps - 1)], hx_recv)
    squares = None
    for s in range(reps):
        v = hx[s].astype(F32)
        part = jnp.sum(v * v, axis=1, keepdims=True)
        squares = part if s == 0 else squares + part
    root = jnp.sqrt(squares / features + EPSILON)
    lax.fori_loop(0, ticks, tick, 0)

    updates = [
        pltpu.make_async_copy(gu, gu_out, o_sem.at[0]),
        pltpu.make_async_copy(uu, uu_out, o_sem.at[1]),
        pltpu.make_async_copy(du, du_out, o_sem.at[2]),
    ]
    for copy in updates:
        copy.start()

    grad = tok[0, :, WIDTH:].astype(F32)

    r = iota((ROWS, 1), 0)
    code = code_of(choose(r & 15, ALL), r >> 4, jnp.full_like(r, 4))
    wait(fifth_in.at[16:64, :], l_recv)
    add_rows(code, fifth_in[...])
    out_rows = [picked[k, :, 0:WIDTH] for k in range(2)]
    share_out = (w[0] * out_rows[0] + w[1] * out_rows[1]).astype(BF16)
    share_in = (picked[0, :, WIDTH:] + picked[1, :, WIDTH:]).astype(BF16)
    def share_out_rows(parts, first):
        rows = slice(share * first, share * (first + len(parts)))
        for s in range(reps):
            for i, part in enumerate(parts):
                fin[s, share * (first + i) : share * (first + i + 1), :] = part[share * s : share * s + share, :]
        for ro in range(1, reps):
            to = fin.at[rid(ro // 2, ro % 2), rows, :]
            send(to, fin_in.at[rep, rows, :], y_send, y_recv, at(ro // 2, ro % 2))

    share_out_rows([share_out[:, 0:128], share_out[:, 128:], share_in[:, 0:128], share_in[:, 128:]], 0)
    dots = [jnp.sum(p * grad, axis=1, keepdims=True) for p in out_rows]
    heads = [d.astype(BF16).astype(F32) for d in dots]
    lane = iota((128, 128), 1)
    products = jnp.where(
        lane == 0, heads[0],
        jnp.where(lane == 1, heads[1], jnp.where(lane == 2, dots[0] - heads[0], jnp.where(lane == 3, dots[1] - heads[1], 0.0))),
    ).astype(BF16)
    share_out_rows([products], 4)
    fin_in[rep] = fin[rep]

    wait(fin_in.at[pl.ds(0, reps - 1)], y_recv)
    inner = route = None
    for s in range(2 * reps):
        cols = slice(128 * s, 128 * s + 128)
        v = hx[s // 2, :, 128 * (s % 2) : 128 * (s % 2) + 128].astype(F32)
        at_out, at_in = share * (s % 2), share * (2 + s % 2)
        lo_ref[:, cols] = (v + fin_in[s // 2, at_out : at_out + share, :].astype(F32)).astype(BF16)
        scaled = gain_ref[:, cols] * fin_in[s // 2, at_in : at_in + share, :].astype(F32)
        part = jnp.sum(scaled * v, axis=1, keepdims=True)
        inner = part if s == 0 else inner + part
    for s in range(reps):
        part = fin_in[s, 4 * share :, :].astype(F32)
        route = part if s == 0 else route + part
    coefficient = inner / (features * root * root * root)
    for s in range(2 * reps):
        cols = slice(128 * s, 128 * s + 128)
        v = hx[s // 2, :, 128 * (s % 2) : 128 * (s % 2) + 128].astype(F32)
        at_in = share * (2 + s % 2)
        scaled = gain_ref[:, cols] * fin_in[s // 2, at_in : at_in + share, :].astype(F32)
        ig_ref[:, cols] = (scaled / root - v * coefficient).astype(BF16)
    diagonal = iota((share, share), 0) == iota((share, share), 1)
    for k in range(2):
        column = route[:, k : k + 1] + route[:, 2 + k : 3 + k]
        rg_ref[k : k + 1, :] = jnp.sum(jnp.where(diagonal, column, 0.0), axis=0, keepdims=True)

    wait(meta.at[1:NJ], meta_send)
    wait(tok.at[1:NJ], tok_send)
    wait(hx.at[pl.ds(0, reps - 1)], hx_send)
    for c in range(CHUNKS):
        sent = slice(0, 240 if c in (HOME, FIFTH) else 256)
        wait(zout.at[c, sent, :], z_send.at[c])
        wait(fout.at[c, sent, :], f_send.at[c])
    for c in range(CHUNKS):
        wait(gat.at[c, pl.ds(0, 7)], c_send.at[c])
        wait(got.at[c], e_send.at[c])
    wait(loc.at[1:NJ], l_send)
    wait(fin.at[pl.ds(0, reps - 1)], y_send)
    for copy in updates:
        copy.wait()


def hand_out(*refs):
    n = (len(refs) - 2) // 3
    sources, results, held, in_sem, out_sem = refs[:n], refs[n : 2 * n], refs[2 * n : 3 * n], refs[-2], refs[-1]
    pieces = [(i, slice(96 * k, 96 * k + 96)) for i in range(3, n) for k in range(2)]
    pieces += [(i, slice(None)) for i in range(3)]
    arriving, leaving = [], []
    for k, (i, rows) in enumerate(pieces):
        arriving.append(pltpu.make_async_copy(sources[i].at[rows, :], held[i].at[rows, :], in_sem.at[k]))
        arriving[-1].start()
    for k, (i, rows) in enumerate(pieces):
        arriving[k].wait()
        leaving.append(pltpu.make_async_copy(held[i].at[rows, :], results[i].at[rows, :], out_sem.at[k]))
        leaving[-1].start()
    for copy in leaving:
        copy.wait()


def body(hidden_in, norm_gain, route_ids, route_weights, w_gate, w_up, w_down, out_grad):
    reps = lax.axis_size("rep")
    units, features = w_gate.shape[1:]
    tokens = hidden_in.shape[0]
    share = tokens // reps
    vmem = pl.BlockSpec(memory_space=pltpu.VMEM)
    hbm = pl.BlockSpec(memory_space=pltpu.HBM)
    anywhere = pl.BlockSpec(memory_space=pl.ANY)
    matrix = pltpu.VMEM((units, features), BF16)
    dma = pltpu.SemaphoreType.DMA
    rows = CHUNKS * ROWS
    scratch = [matrix] * 6 + [
        pltpu.VMEM((2, tokens), jnp.int32),
        pltpu.VMEM((2, tokens), F32),
        pltpu.VMEM((1, features), F32),
        pltpu.VMEM((4, ROWS, 4 * ROWS), BF16),
        pltpu.VMEM((NJ, tokens, 2 * WIDTH), BF16),
        pltpu.VMEM((NJ, 8, tokens), F32),
        pltpu.VMEM((reps, share, WIDTH), BF16),
        pltpu.VMEM((CHUNKS, 4 * ROWS, 128), BF16),
        pltpu.VMEM((CHUNKS, 4 * ROWS, 128), BF16),
        pltpu.VMEM((CHUNKS, reps, ROWS, 2 * WIDTH), BF16),
        pltpu.VMEM((CHUNKS, ROWS, features), BF16),
        pltpu.VMEM((CHUNKS, reps, ROWS, 2 * WIDTH), BF16),
        pltpu.VMEM((CHUNKS, 7, ROWS, 2 * WIDTH), BF16),
        pltpu.VMEM((CHUNKS, 4 * ROWS, 128), BF16),
        pltpu.VMEM((CHUNKS, 4 * ROWS, 128), BF16),
        pltpu.VMEM((NJ, 16, 2 * WIDTH), BF16),
        pltpu.VMEM((ROWS, 2 * WIDTH), BF16),
        pltpu.VMEM((2, tokens, 2 * WIDTH), F32),
        pltpu.VMEM((reps, 5 * share, 128), BF16),
        pltpu.VMEM((reps, 5 * share, 128), BF16),
    ]
    scratch += [pltpu.VMEM((CHUNKS, ROWS, units), BF16)] * 3
    scratch += [pltpu.VMEM((units, rows), BF16)] * 3
    scratch += [
        dma((3,)), dma((3,)), dma((5,)),
        dma, dma, dma, dma((3,)),
        dma, dma,
        dma((CHUNKS,)), dma((CHUNKS,)),
        dma((CHUNKS,)), dma((CHUNKS, 8)),
        dma((CHUNKS,)), dma((CHUNKS, 8)),
        dma((CHUNKS,)), dma((CHUNKS,)),
        dma, dma,
        dma, dma,
    ]
    update = jax.ShapeDtypeStruct((units, features), BF16)
    kinds = (
        jax.ShapeDtypeStruct((share, features), BF16),
        jax.ShapeDtypeStruct((share, features), BF16),
        jax.ShapeDtypeStruct((2, share), F32),
        update, update, update,
    )
    outs = pl.pallas_call(
        kernel,
        out_shape=kinds,
        in_specs=[hbm] * 8,
        out_specs=(vmem, vmem, vmem, anywhere, anywhere, anywhere),
        scratch_shapes=scratch,
        compiler_params=pltpu.CompilerParams(
            collective_id=0, has_side_effects=True, vmem_limit_bytes=62 * 1024 * 1024
        ),
        name="expert_layer",
    )(
        hidden_in, out_grad, route_ids.T, route_weights.T, norm_gain[None, :], w_gate[0], w_up[0], w_down[0]
    )
    outs = pl.pallas_call(
        hand_out,
        out_shape=kinds,
        in_specs=[anywhere] * 6,
        out_specs=(anywhere,) * 6,
        scratch_shapes=[pltpu.VMEM(kind.shape, kind.dtype) for kind in kinds] + [dma((9,)), dma((9,))],
        name="results",
    )(*outs)
    layer_out, input_grad, route_grad, gate_update, up_update, down_update = outs
    return layer_out, input_grad, route_grad.T, gate_update[None], up_update[None], down_update[None]


def solution(mesh):
    placed = (
        P("exp", "rep"),
        P(),
        P("exp", None),
        P("exp", None),
        P("exp", "rep", None),
        P("exp", "rep", None),
        P("exp", "rep", None),
        P("exp", "rep"),
    )
    return jax.shard_map(
        body,
        mesh=mesh,
        in_specs=placed,
        out_specs=(
            P(("exp", "rep"), None),
            P(("exp", "rep"), None),
            P(("exp", "rep"), None),
            P("exp", "rep", None),
            P("exp", "rep", None),
            P("exp", "rep", None),
        ),
        check_vma=False,
    )
```
